512 devices in a mesh: tan: 16 (over z), rad: 16 (over x_lo, y, core), inst: 2 (over x_hi).
Axes of the slice: x: 4 (x_hi: 2, x_lo: 2; x = x_hi * 2 + x_lo), y: 4, z: 16, core: 2. Of those that a mesh axis runs over, the one named last changes fastest.
Arguments:
- coords: float32 [2, 3, 512, 8, 2048], P('inst', None, 'rad', None, 'tan'), may hold values from -533 to 533, as said below
- state: float32 [2, 5, 512, 8, 2048], P('inst', None, 'rad', None, 'tan'), may hold values from -6 to 6
- spectral_rest: float32 [2, 5, 512, 8, 2048], P('inst', None, 'rad', None, 'tan'), may hold values from -4 to 4
- instance_ids: int32 [2], replicated, may hold values from 0 to 15, as said below
- motion: float32 [2], replicated, may hold values from 0.2 to 0.6
- heave: float32 [3], replicated, may hold values from -3 to 3
- free_stream: float32 [3], replicated, may hold values from -3 to 3
Outputs:
- displacement: float32 [2, 3, 512, 8, 2048], P('inst', None, 'rad', None, 'tan')
- residual: float32 [2, 5, 512, 8, 2048], P('inst', None, 'rad', None, 'tan')
The draws below stay inside these ranges and needn't reach their ends.
Inputs may be any that keep to these rules, and one draw needn't show every extreme that they name: `instance_ids`: one of the two instance numbers is 15; the other lies 1 to 3 instances away from it, modulo 16. `coords`: points of an O-grid around a body, radial distance rising along j.
All inputs are finite; a program needn't handle non-finite values.
Results may differ from the reference program's by a relative error of at most 0.0003.
Values sent between devices are 32-bit elements; how exact they have to be, the bound alone decides.
A program may use at most 64 MiB of HBM per device.

```python
import jax
import jax.numpy as jnp
from jax import lax

SPAN = 8
NINST = 16
WINDOW = 2
NR = 512
NT = 2048


radius_base = 20.0


def draw_coords(key, part):
    key = jax.random.fold_in(key, 11)
    key_rad, key_tan, key_span = jax.random.split(key, 3)
    shape = (WINDOW, NR, SPAN, NT)
    jitter_rad = jax.random.uniform(key_rad, shape, jnp.float32)
    jitter_tan = jax.random.uniform(key_tan, shape, jnp.float32)
    jitter_span = jax.random.uniform(key_span, shape, jnp.float32)
    radius = radius_base + jnp.arange(NR, dtype=jnp.float32)[None, :, None, None] + 0.45 * jitter_rad
    angle = 2.0 * jnp.pi * (jnp.arange(NT, dtype=jnp.float32)[None, None, None, :] + 0.3 * jitter_tan) / NT
    height = jnp.arange(SPAN, dtype=jnp.float32)[None, None, :, None] + 0.3 * jitter_span
    points = jnp.stack([radius * jnp.cos(angle), radius * jnp.sin(angle), height], axis=1)
    return points.astype(jnp.float32)


def draw_instance_ids(key, part):
    key = jax.random.fold_in(key, 23)
    key_gap, key_side, key_order = jax.random.split(key, 3)
    gap = jax.random.randint(key_gap, (), 1, 4)
    side = jax.random.randint(key_side, (), 0, 2)
    order = jax.random.randint(key_order, (), 0, 2)
    last = jnp.int32(NINST - 1)
    other = jnp.where(side == 0, last - gap, gap - 1)
    first = jnp.where(order == 0, last, other)
    second = jnp.where(order == 0, other, last)
    return jnp.stack([first, second]).astype(jnp.int32)


def block_levels(own_key, shape, pieces, least, high):
    factor_of, own = 1.0, jax.random.fold_in(own_key, 6)
    for axis_at, blocks in pieces:
        draws = jnp.exp(jax.random.uniform(jax.random.fold_in(own, axis_at), (blocks,), jnp.float32, least / len(pieces), high / len(pieces)))
        factor_of = factor_of * jnp.repeat(draws, shape[axis_at] // blocks).reshape([-1 if axis == axis_at else 1 for axis in range(len(shape))])
    return factor_of


def gaussian(rng, shape, width, bound, cuts=(), held_as=jnp.bfloat16):
    values = width * jax.random.normal(rng, shape, jnp.float32)
    if cuts:
        values = values * block_levels(rng, shape, cuts, -0.22, 0.18)
    return jnp.clip(values, -bound, bound).astype(held_as)


def setup_inputs(seed: int = 0) -> dict:
    seeds = jax.random.split(jax.random.key(seed), 8)
    coords = draw_coords(jax.random.fold_in(seeds[7], 71), 0)
    state = gaussian(seeds[1], (WINDOW, 5, NR, SPAN, NT), 1.0, 6.0, ((0, 2), (2, 16), (4, 16)), jnp.float32)
    spectral_rest = gaussian(seeds[2], (WINDOW, 5, NR, SPAN, NT), 0.5, 4.0, ((0, 2), (2, 16), (4, 16)), jnp.float32)
    instance_ids = draw_instance_ids(jax.random.fold_in(seeds[7], 71), 0)
    motion = jnp.clip(jax.random.uniform(seeds[4], (2,), jnp.float32, 0.2, 0.6), 0.2, 0.6)
    heave = gaussian(seeds[5], (3,), 1.0, 3.0, (), jnp.float32)
    free_stream = gaussian(seeds[6], (3,), 1.0, 3.0, (), jnp.float32)
    return dict(coords=coords, state=state, spectral_rest=spectral_rest, instance_ids=instance_ids, motion=motion, heave=heave, free_stream=free_stream)


coef_two = 0.1
coef_four = 0.05

def shift_rad(field, offset):
    padded = jnp.pad(field, ((0, 0), (2, 2), (0, 0), (0, 0)))
    return padded[:, 2 + offset:2 + offset + field.shape[1]]

def shift_tan(field, offset):
    return jnp.roll(field, -offset, axis=3)

def axis_slope(field, axis):
    count = field.shape[axis]
    first = lax.slice_in_dim(field, 1, 2, axis=axis) - lax.slice_in_dim(field, 0, 1, axis=axis)
    middle = (lax.slice_in_dim(field, 2, count, axis=axis) - lax.slice_in_dim(field, 0, count - 2, axis=axis)) * 0.5
    last = lax.slice_in_dim(field, count - 1, count, axis=axis) - lax.slice_in_dim(field, count - 2, count - 1, axis=axis)
    return jnp.concatenate([first, middle, last], axis=axis)

def triple(rad_vec, tan_vec, span_vec):
    return rad_vec[0] * (tan_vec[1] * span_vec[2] - tan_vec[2] * span_vec[1]) + rad_vec[1] * (tan_vec[2] * span_vec[0] - tan_vec[0] * span_vec[2]) + rad_vec[2] * (tan_vec[0] * span_vec[1] - tan_vec[1] * span_vec[0])

def jst_term(minus_two, minus_one, centre, plus_one, plus_two, speed):
    press_minus = 1.0 + minus_one[0] * minus_one[0]
    press_centre = 1.0 + centre[0] * centre[0]
    press_plus = 1.0 + plus_one[0] * plus_one[0]
    sensor = coef_two * jnp.abs(press_plus - 2.0 * press_centre + press_minus) / (press_plus + 2.0 * press_centre + press_minus)
    fourth = jnp.maximum(0.0, coef_four - sensor)
    second_diff = plus_one - 2.0 * centre + minus_one
    fourth_diff = plus_two - 4.0 * plus_one + 6.0 * centre - 4.0 * minus_one + minus_two
    return speed * 0.5 * (plus_one - minus_one) - jnp.abs(speed) * (sensor * second_diff - fourth * fourth_diff)

def spectral_coef(offset):
    angle = jnp.pi * offset.astype(jnp.float32) / NINST
    parity = 1.0 - 2.0 * (offset % 2).astype(jnp.float32)
    return 0.5 * parity * jnp.cos(angle) / jnp.sin(angle)

def reference(coords, state, spectral_rest, instance_ids, motion, heave, free_stream):
    moves = []
    volumes = []
    tangents = []
    radials = []
    for member in range(WINDOW):
        grid = coords[member]
        below = shift_rad(grid, -1)
        seg = jnp.sqrt(lax.optimization_barrier(jnp.sum((grid - below) ** 2, axis=0)))
        layer = jnp.arange(NR)[:, None, None]
        seg = jnp.where(layer == 0, 0.0, seg)
        cumul = jnp.cumsum(seg, axis=0)
        frac = cumul / cumul[-1:]
        phase = 2.0 * jnp.pi * instance_ids[member].astype(jnp.float32) / NINST + motion[1]
        theta = motion[0] * jnp.sin(phase)
        wall = grid[:, 0]
        wall_y = wall[1] * jnp.cos(theta) - wall[2] * jnp.sin(theta) - wall[1]
        wall_z = wall[1] * jnp.sin(theta) + wall[2] * jnp.cos(theta) - wall[2]
        wall_disp = jnp.stack([jnp.zeros_like(wall_y), wall_y, wall_z])
        far = heave * jnp.cos(phase)
        disp = (1.0 - frac)[None] * wall_disp[:, None] + frac[None] * far[:, None, None, None]
        moved = grid + disp
        tan_vec = (shift_tan(moved, 1) - shift_tan(moved, -1)) * 0.5
        rad_vec = axis_slope(moved, 1)
        span_vec = axis_slope(moved, 2)
        moves.append(disp)
        volumes.append(triple(rad_vec, tan_vec, span_vec))
        tangents.append(tan_vec)
        radials.append(rad_vec)
    results = []
    for member in range(WINDOW):
        other = WINDOW - 1 - member
        coef = spectral_coef(instance_ids[member] - instance_ids[other])
        relative = free_stream[:, None, None, None] - coef * moves[other]
        speed_tan = lax.optimization_barrier(jnp.sum(relative * tangents[member], axis=0))
        speed_rad = lax.optimization_barrier(jnp.sum(relative * radials[member], axis=0))
        flow = state[member]
        term_tan = jst_term(shift_tan(flow, -2), shift_tan(flow, -1), flow, shift_tan(flow, 1), shift_tan(flow, 2), speed_tan)
        term_rad = jst_term(shift_rad(flow, -2), shift_rad(flow, -1), flow, shift_rad(flow, 1), shift_rad(flow, 2), speed_rad)
        weighted = volumes[other][None] * state[other]
        results.append(term_tan + term_rad + coef * weighted + spectral_rest[member])
    return (jnp.stack(moves), jnp.stack(results))
```

```python
import functools

import jax
import jax.numpy as jnp
from jax import lax
from jax.experimental import pallas as pl
from jax.experimental.pallas import tpu as pltpu
from jax.sharding import PartitionSpec as P

NINST = 16
COEF_TWO = 0.1
COEF_FOUR = 0.05
MESH = pl.DeviceIdType.MESH
ROWS = 32
CHUNKS = 4
TILE = (8, 128)


def send(src, dst, sems, slot, device):
    return pltpu.make_async_remote_copy(
        src_ref=src,
        dst_ref=dst,
        send_sem=sems[0].at[slot],
        recv_sem=sems[1].at[slot],
        device_id=device,
        device_id_type=MESH,
    )


def length(a, b):
    d = [p - q for p, q in zip(a, b)]
    return jnp.sqrt(d[0] * d[0] + d[1] * d[1] + d[2] * d[2])


def jst(m2, m1, c, p1, p2, speed):
    q_m, q_c, q_p = (1.0 + w[0] * w[0] for w in (m1, c, p1))
    outer = q_p + q_m
    sensor = COEF_TWO * jnp.abs(outer - 2.0 * q_c) / (outer + 2.0 * q_c)
    fourth = jnp.maximum(0.0, COEF_FOUR - sensor)
    size = jnp.abs(speed)
    half = 0.5 * speed
    near = size * (sensor + 4.0 * fourth)
    mid = size * (2.0 * sensor + 6.0 * fourth)
    far = size * fourth
    return [
        half * (p1[k] - m1[k]) - near * (p1[k] + m1[k]) + mid * c[k] + far * (p2[k] + m2[k])
        for k in range(5)
    ]


def step_kernel(
    nrad, ntan,
    coords, state, rest, ids, motion, heave, stream,
    disp_out, res_out,
    grid, flow, rest_v, moved, arc, frac_out, frac_in, e_t, e_r, vol_out, vol_in, state_in,
    wall, sums, cross_out, cross_in, flow_edge, flow_left, flow_right, move_edge, move_left, move_right,
    ids_s, motion_s, heave_s, stream_s,
    local, bulk_s, bulk_r, row_s, row_r, wall_s, wall_r, sum_s, sum_r, one_s, one_r,
):
    rad, tan, inst = lax.axis_index("rad"), lax.axis_index("tan"), lax.axis_index("inst")
    half = nrad // 2
    place, side = lax.rem(rad, half), rad // half
    first, last = rad == 0, rad == nrad - 1
    partner = {"inst": 1 - inst}
    left = {"tan": lax.rem(tan + ntan - 1, ntan)}
    right = {"tan": lax.rem(tan + 1, ntan)}
    above = {"rad": lax.rem(rad + 1, nrad)}
    below = {"rad": lax.rem(rad + nrad - 1, nrad)}
    across = {"rad": lax.rem(rad + half, nrad)}
    peers = [{"rad": side * half + lax.rem(place + k, half)} for k in range(1, half)]

    loads = [
        pltpu.make_async_copy(coords.at[0], grid.at[:, pl.ds(1, ROWS)], local.at[0]),
        pltpu.make_async_copy(state.at[0], flow.at[:, pl.ds(2, ROWS)], local.at[1]),
        pltpu.make_async_copy(rest.at[0], rest_v, local.at[2]),
        pltpu.make_async_copy(ids, ids_s, local.at[3]),
        pltpu.make_async_copy(motion, motion_s, local.at[4]),
        pltpu.make_async_copy(heave, heave_s, local.at[5]),
        pltpu.make_async_copy(stream, stream_s, local.at[6]),
    ]
    barrier = pltpu.get_barrier_semaphore()
    for device in [partner, left, right, across] + peers:
        pl.semaphore_signal(barrier, inc=1, device_id=device, device_id_type=MESH)

    @pl.when(rad == half - 1)
    def _():
        pl.semaphore_signal(barrier, inc=1, device_id=above, device_id_type=MESH)

    @pl.when(rad == half)
    def _():
        pl.semaphore_signal(barrier, inc=1, device_id=below, device_id_type=MESH)

    for load in loads:
        load.start()
    beyond = jnp.where((rad == half - 1) | (rad == half), 1, 0)
    pl.semaphore_wait(barrier, 4 + half - 1 + beyond)

    row = (row_s, row_r)
    to_above = [
        send(coords.at[0, :, ROWS - 1], grid.at[:, 0], row, 0, above),
        send(state.at[0, :, pl.ds(ROWS - 2, 2)], flow.at[:, pl.ds(0, 2)], row, 1, above),
    ]
    to_below = [
        send(coords.at[0, :, 0], grid.at[:, ROWS + 1], row, 2, below),
        send(state.at[0, :, pl.ds(0, 2)], flow.at[:, pl.ds(ROWS + 2, 2)], row, 3, below),
    ]
    walls = [
        send(coords.at[0, pl.ds(1, 2), 0], wall, (wall_s, wall_r), k, device)
        for k, device in enumerate([across] + peers)
    ]
    passed = [send(wall, wall, (wall_s, wall_r), k + 1, device) for k, device in enumerate(peers)]
    count = ROWS // CHUNKS
    bulk = [
        send(
            state.at[0, :, pl.ds(k * count, count)],
            state_in.at[:, pl.ds(k * count, count)],
            (bulk_s, bulk_r), k, partner,
        )
        for k in range(CHUNKS)
    ]

    @pl.when(rad < nrad - 1)
    def _():
        to_above[0].start()

    @pl.when(rad > 0)
    def _():
        to_below[0].start()

    @pl.when(first)
    def _():
        for copy in walls:
            copy.start()

    @pl.when(rad < nrad - 1)
    def _():
        to_above[1].start()

    @pl.when(rad > 0)
    def _():
        to_below[1].start()

    for copy in bulk:
        copy.start()

    lane = lax.broadcasted_iota(jnp.int32, TILE, 1)
    span = lax.broadcasted_iota(jnp.int32, TILE, 0)
    zero = jnp.zeros(TILE, jnp.float32)

    loads[0].wait()

    def inner(j, carry):
        before, total = carry[:3], carry[3]
        here = tuple(grid[c, j + 1] for c in range(3))
        total = total + length(here, before)
        arc[j] = total
        return (*here, total)

    arc[0] = zero
    top = lax.fori_loop(
        1, ROWS, inner, (*(grid[c, 1] for c in range(3)), zero), unroll=4
    )

    loads[1].wait()

    def pack_flow(j, edge):
        mine = lane // 4 == j
        return tuple(
            jnp.where(mine, pltpu.roll(flow[c, j + 2], 4 * j + 2, 1), edge[c]) for c in range(5)
        )

    edges = lax.fori_loop(0, ROWS, pack_flow, (zero,) * 5, unroll=4)
    for c in range(5):
        flow_edge[c] = edges[c]
    one = (one_s, one_r)
    flow_sends = [
        send(flow_edge, flow_left, one, 0, right),
        send(flow_edge, flow_right, one, 1, left),
    ]
    for copy in flow_sends:
        copy.start()

    for load in loads[3:]:
        load.wait()
    own_id = jnp.where(inst == 0, ids_s[0], ids_s[1])
    other_id = jnp.where(inst == 0, ids_s[1], ids_s[0])
    offset_id = own_id - other_id
    turn = 2.0 * jnp.pi / NINST
    own_phase = turn * own_id.astype(jnp.float32) + motion_s[1]
    other_phase = turn * other_id.astype(jnp.float32) + motion_s[1]
    angle = (jnp.pi / NINST) * offset_id.astype(jnp.float32)
    angles = jnp.where(span == 0, own_phase, jnp.where(span == 1, other_phase, angle))
    sines, cosines = jnp.sin(angles), jnp.cos(angles)

    def pick(values, k):
        return jnp.broadcast_to(values[k : k + 1], TILE)

    theta = motion_s[0] * pick(sines, 0)
    sin_theta, cos_theta = jnp.sin(theta), jnp.cos(theta)
    own_far = [heave_s[c] * pick(cosines, 0) for c in range(3)]
    other_far = [heave_s[c] * pick(cosines, 1) for c in range(3)]
    parity = 1.0 - 2.0 * lax.rem(offset_id + NINST, 2).astype(jnp.float32)
    coef = 0.5 * parity * pick(cosines, 2) / pick(sines, 2)

    @pl.when(rad > 0)
    def _():
        to_above[0].wait_recv()

    @pl.when(first)
    def _():
        for c in range(3):
            grid[c, 0] = grid[c, 1]

    step_in = length([grid[c, 1] for c in range(3)], [grid[c, 0] for c in range(3)])
    line = step_in + top[3]
    sums[place] = line
    sum_sends = [
        send(sums.at[place], sums.at[place], (sum_s, sum_r), k, device)
        for k, device in enumerate(peers)
    ]
    for copy in sum_sends:
        copy.start()

    @pl.when(rad == half)
    def _():
        walls[0].wait_recv()
        for copy in passed:
            copy.start()

    for copy in sum_sends:
        copy.wait_recv()
    own_half, lower = zero, zero
    for k in range(half):
        part = sums[k]
        own_half = own_half + part
        lower = lower + jnp.where(k < place, part, 0.0)
    cross_out[...] = own_half
    cross = send(cross_out, cross_in, one, 2, across)
    cross.start()

    @pl.when(first)
    def _():
        for c in range(2):
            wall[c] = grid[c + 1, 1]

    @pl.when((rad != 0) & (rad != half))
    def _():
        for k in range(half - 1):

            @pl.when(place == k + 1)
            def _():
                walls[k + 1].wait_recv()

    @pl.when(rad < nrad - 1)
    def _():
        to_below[0].wait_recv()

    @pl.when(last)
    def _():
        for c in range(3):
            grid[c, ROWS + 1] = grid[c, ROWS]

    step_out = length([grid[c, ROWS + 1] for c in range(3)], [grid[c, ROWS] for c in range(3)])
    wall_y, wall_z = wall[0], wall[1]
    own_wall = [
        zero,
        wall_y * cos_theta - wall_z * sin_theta - wall_y,
        wall_y * sin_theta + wall_z * cos_theta - wall_z,
    ]
    frac_out[ROWS] = own_wall[1]
    frac_out[ROWS + 1] = own_wall[2]

    cross.wait_recv()
    other_half = cross_in[...]
    inverse = 1.0 / (own_half + other_half)
    offset = lower + jnp.where(side == 1, other_half, 0.0)
    base = offset + step_in

    def displaced(frac):
        return [
            frac * own_far[0],
            (1.0 - frac) * own_wall[1] + frac * own_far[1],
            (1.0 - frac) * own_wall[2] + frac * own_far[2],
        ]

    def move(j, edge):
        frac = (base + arc[j]) * inverse
        frac_out[j] = frac
        mine = lane // 2 == j
        out = []
        for c, d in enumerate(displaced(frac)):
            disp_out[c, j] = d
            point = grid[c, j + 1] + d
            moved[c, j + 1] = point
            out.append(jnp.where(mine, pltpu.roll(point, 2 * j + 1, 1), edge[c]))
        return tuple(out)

    edges = lax.fori_loop(0, ROWS, move, (zero,) * 3, unroll=4)
    for c in range(3):
        move_edge[c] = edges[c]
    move_sends = [
        send(move_edge, move_left, one, 3, right),
        send(move_edge, move_right, one, 4, left),
    ]
    for copy in move_sends:
        copy.start()
    frac_send = send(frac_out, frac_in, one, 5, partner)
    frac_send.start()

    for c, d in enumerate(displaced(offset * inverse)):
        moved[c, 0] = grid[c, 0] + d
    for c, d in enumerate(displaced((base + top[3] + step_out) * inverse)):
        moved[c, ROWS + 1] = grid[c, ROWS + 1] + d

    @pl.when(first)
    def _():
        for c in range(3):
            moved[c, 0] = moved[c, 1]

    @pl.when(last)
    def _():
        for c in range(3):
            moved[c, ROWS + 1] = moved[c, ROWS]

    for copy in move_sends:
        copy.wait_recv()
    even = lax.rem(lane, 2) == 0
    beside = [jnp.where(even, move_left[c], move_right[c]) for c in range(3)]
    at_low, at_high = span == 0, span == 7
    span_scale = jnp.where(at_low | at_high, 1.0, 0.5)

    def slopes(j, carry):
        one_sided = (first & (j == 0)) | (last & (j == ROWS - 1))
        scale = jnp.where(one_sided, 1.0, 0.5)
        t, r, z = [], [], []
        for c in range(3):
            here = moved[c, j + 1]
            out = pltpu.roll(beside[c], lax.rem(127 - 2 * j, 128), 1)
            ahead = pltpu.roll(jnp.where(lane == 0, out, here), 127, 1)
            behind = pltpu.roll(jnp.where(lane == 127, out, here), 1, 1)
            t.append((ahead - behind) * 0.5)
            r.append((moved[c, j + 2] - moved[c, j]) * scale)
            over = jnp.where(at_high, here, pltpu.roll(here, 7, 0))
            under = jnp.where(at_low, here, pltpu.roll(here, 1, 0))
            z.append((over - under) * span_scale)
            e_t[c, j] = t[c]
            e_r[c, j] = r[c]
        vol_out[j] = (
            r[0] * (t[1] * z[2] - t[2] * z[1])
            + r[1] * (t[2] * z[0] - t[0] * z[2])
            + r[2] * (t[0] * z[1] - t[1] * z[0])
        )
        return carry

    lax.fori_loop(0, ROWS, slopes, 0, unroll=2)
    vol_send = send(vol_out, vol_in, one, 6, partner)
    vol_send.start()

    @pl.when(rad > 0)
    def _():
        to_above[1].wait_recv()

    @pl.when(first)
    def _():
        flow[:, 0:2] = jnp.zeros((5, 2, *TILE), jnp.float32)

    @pl.when(rad < nrad - 1)
    def _():
        to_below[1].wait_recv()

    @pl.when(last)
    def _():
        flow[:, ROWS + 2 : ROWS + 4] = jnp.zeros((5, 2, *TILE), jnp.float32)

    for copy in flow_sends:
        copy.wait_recv()
    loads[2].wait()
    frac_send.wait_recv()
    low = lax.rem(lane, 4) < 2
    for c in range(5):
        flow_left[c] = jnp.where(low, flow_left[c], flow_right[c])
    other_wall = [zero, frac_in[ROWS], frac_in[ROWS + 1]]
    start = [stream_s[c] - coef * other_wall[c] for c in range(3)]
    slope = [coef * (other_wall[c] - other_far[c]) for c in range(3)]

    def fluxes(j, carry):
        frac = frac_in[j]
        relative = [start[c] + frac * slope[c] for c in range(3)]
        speed_t = sum(relative[c] * e_t[c, j] for c in range(3))
        speed_r = sum(relative[c] * e_r[c, j] for c in range(3))
        rows = [[flow[c, j + k] for c in range(5)] for k in range(5)]
        here = rows[2]
        shift = lax.rem(126 - 4 * j, 128)
        out = [pltpu.roll(flow_left[c], shift, 1) for c in range(5)]
        m2 = [pltpu.roll(jnp.where(lane >= 126, out[c], here[c]), 2, 1) for c in range(5)]
        m1 = [pltpu.roll(jnp.where(lane == 127, out[c], here[c]), 1, 1) for c in range(5)]
        p1 = [pltpu.roll(jnp.where(lane == 0, out[c], here[c]), 127, 1) for c in range(5)]
        p2 = [pltpu.roll(jnp.where(lane <= 1, out[c], here[c]), 126, 1) for c in range(5)]
        term_t = jst(m2, m1, here, p1, p2, speed_t)
        term_r = jst(*rows, speed_r)
        for c in range(5):
            res_out[c, j] = term_t[c] + term_r[c] + rest_v[c, j]
        return carry

    lax.fori_loop(0, ROWS, fluxes, 0)

    vol_send.wait_recv()
    for k in range(CHUNKS):
        bulk[k].wait_recv()

        def add(j, carry):
            weight = coef * vol_in[j]
            for c in range(5):
                res_out[c, j] = res_out[c, j] + weight * state_in[c, j]
            return carry

        lax.fori_loop(k * count, (k + 1) * count, add, 0, unroll=2)

    @pl.when(rad < nrad - 1)
    def _():
        for copy in to_above:
            copy.wait_send()

    @pl.when(rad > 0)
    def _():
        for copy in to_below:
            copy.wait_send()

    @pl.when(first)
    def _():
        for copy in walls:
            copy.wait_send()

    @pl.when(rad == half)
    def _():
        for copy in passed:
            copy.wait_send()

    for copy in flow_sends + sum_sends + [cross] + move_sends + [frac_send, vol_send] + bulk:
        copy.wait_send()


def store_kernel(disp, res, disp_out, res_out, sems):
    copies = [
        pltpu.make_async_copy(disp, disp_out.at[0], sems.at[0]),
        pltpu.make_async_copy(res, res_out.at[0], sems.at[1]),
    ]
    for copy in copies:
        copy.start()
    for copy in copies:
        copy.wait()


def body(nrad, ntan, *args):
    half = nrad // 2
    f32 = jnp.float32
    vmem, hbm = pltpu.VMEM, pltpu.HBM

    def tiles(*lead):
        return pltpu.VMEM((*lead, *TILE), f32)

    dma = pltpu.SemaphoreType.DMA
    scratch = [
        tiles(3, ROWS + 2), tiles(5, ROWS + 4), tiles(5, ROWS), tiles(3, ROWS + 2), tiles(ROWS),
        tiles(ROWS + 2), tiles(ROWS + 2), tiles(3, ROWS), tiles(3, ROWS), tiles(ROWS), tiles(ROWS),
        tiles(5, ROWS), tiles(2), tiles(half), tiles(), tiles(),
        tiles(5), tiles(5), tiles(5), tiles(3), tiles(3), tiles(3),
        pltpu.SMEM((2,), jnp.int32), pltpu.SMEM((2,), f32), pltpu.SMEM((3,), f32), pltpu.SMEM((3,), f32),
        dma((7,)), dma((CHUNKS,)), dma((CHUNKS,)), dma((4,)), dma((4,)),
        dma((half,)), dma((half,)), dma((half - 1,)), dma((half - 1,)), dma((7,)), dma((7,)),
    ]
    disp, res = pl.pallas_call(
        functools.partial(step_kernel, nrad, ntan),
        out_shape=[
            jax.ShapeDtypeStruct((3, ROWS, *TILE), f32),
            jax.ShapeDtypeStruct((5, ROWS, *TILE), f32),
        ],
        in_specs=[pl.BlockSpec(memory_space=hbm)] * 7,
        out_specs=[pl.BlockSpec(memory_space=vmem)] * 2,
        scratch_shapes=scratch,
        name="deform_and_residual",
        compiler_params=pltpu.CompilerParams(
            collective_id=0, has_side_effects=True, vmem_limit_bytes=24 * 2**20
        ),
    )(*(pltpu.with_memory_space_constraint(arg, hbm) for arg in args))
    return pl.pallas_call(
        store_kernel,
        out_shape=[
            jax.ShapeDtypeStruct((1, 3, ROWS, *TILE), f32),
            jax.ShapeDtypeStruct((1, 5, ROWS, *TILE), f32),
        ],
        in_specs=[pl.BlockSpec(memory_space=vmem)] * 2,
        out_specs=[pl.BlockSpec(memory_space=hbm)] * 2,
        scratch_shapes=[dma((2,))],
        name="store_results",
    )(disp, res)


def solution(mesh):
    split = P("inst", None, "rad", None, "tan")
    return jax.shard_map(
        functools.partial(body, mesh.shape["rad"], mesh.shape["tan"]),
        mesh=mesh,
        in_specs=(split, split, split, P(), P(), P(), P()),
        out_specs=(split, split),
        check_vma=False,
    )
```

```python
import functools

import jax
import jax.numpy as jnp
from jax import lax
from jax.experimental import pallas as pl
from jax.experimental.pallas import tpu as pltpu
from jax.sharding import PartitionSpec as P

NINST = 16
COEF_TWO = 0.1
COEF_FOUR = 0.05
MESH = pl.DeviceIdType.MESH
ROWS = 32
CHUNKS = 8
PARTS = 4
TILE = (8, 128)


def send(src, dst, sems, slot, device):
    return pltpu.make_async_remote_copy(
        src_ref=src,
        dst_ref=dst,
        send_sem=sems[0].at[slot],
        recv_sem=sems[1].at[slot],
        device_id=device,
        device_id_type=MESH,
    )


def length(a, b):
    d = [p - q for p, q in zip(a, b)]
    return jnp.sqrt(d[0] * d[0] + d[1] * d[1] + d[2] * d[2])


def each_row(body, carry):
    for j in range(ROWS):
        carry = body(j, carry)
    return carry


def jst(m2, m1, c, p1, p2):
    q_m, q_c, q_p = (1.0 + w[0] * w[0] for w in (m1, c, p1))
    outer = q_p + q_m
    sensor = COEF_TWO * jnp.abs(outer - 2.0 * q_c) / (outer + 2.0 * q_c)
    fourth = jnp.maximum(0.0, COEF_FOUR - sensor)
    near = sensor + 4.0 * fourth
    mid = 2.0 * sensor + 6.0 * fourth
    odd = [0.5 * (p1[k] - m1[k]) for k in range(5)]
    even = [near * (p1[k] + m1[k]) - mid * c[k] - fourth * (p2[k] + m2[k]) for k in range(5)]
    return odd, even


def step_kernel(
    nrad, ntan,
    coords, state, rest, ids, motion, heave, stream,
    disp_out, res_out,
    grid, flow, rest_v, moved, arc, frac_out, frac_in, e_t, e_r, vol_out, vol_in, state_in,
    odd_t, even_t, odd_r, even_r,
    wall, sums, cross_out, cross_in, edge_out, edge_left, edge_right, rim_out, rim_in,
    ids_s, motion_s, heave_s, stream_s,
    local, bulk_s, bulk_r, row_s, row_r, wall_s, wall_r, sum_s, sum_r, one_s, one_r,
    frac_s, frac_r, vol_s, vol_r, ready_right, ready_left,
):
    rad, tan, inst = lax.axis_index("rad"), lax.axis_index("tan"), lax.axis_index("inst")
    half = nrad // 2
    place, side = lax.rem(rad, half), rad // half
    first, last = rad == 0, rad == nrad - 1
    partner = {"inst": 1 - inst}
    left = {"tan": lax.rem(tan + ntan - 1, ntan)}
    right = {"tan": lax.rem(tan + 1, ntan)}
    above = {"rad": lax.rem(rad + 1, nrad)}
    below = {"rad": lax.rem(rad + nrad - 1, nrad)}
    across = {"rad": lax.rem(rad + half, nrad)}
    peers = [{"rad": side * half + lax.rem(place + k, half)} for k in range(1, half)]

    loads = [
        pltpu.make_async_copy(coords.at[0], grid.at[:, pl.ds(1, ROWS)], local.at[0]),
        pltpu.make_async_copy(state.at[0], flow.at[:, pl.ds(2, ROWS)], local.at[1]),
        pltpu.make_async_copy(rest.at[0], rest_v, local.at[2]),
        pltpu.make_async_copy(ids, ids_s, local.at[3]),
        pltpu.make_async_copy(motion, motion_s, local.at[4]),
        pltpu.make_async_copy(heave, heave_s, local.at[5]),
        pltpu.make_async_copy(stream, stream_s, local.at[6]),
    ]
    barrier = pltpu.get_barrier_semaphore()

    def greet(device):
        pl.semaphore_signal(barrier, inc=1, device_id=device, device_id_type=MESH)

    for device in [partner, across] + peers:
        greet(device)
    pl.when(rad == half - 1)(lambda: greet(above))
    pl.when(rad == half)(lambda: greet(below))
    pl.when(tan < ntan - 1)(lambda: greet(right))
    pl.when(tan == 0)(lambda: greet(left))
    for load in loads:
        load.start()

    lane = lax.broadcasted_iota(jnp.int32, TILE, 1)
    span = lax.broadcasted_iota(jnp.int32, TILE, 0)
    zero = jnp.zeros(TILE, jnp.float32)
    row_of, slot = lane // 4, lax.rem(lane, 4)

    loads[0].wait()

    def inner(j, carry):
        before, total = carry[:3], carry[3]
        here = tuple(grid[c, j + 1] for c in range(3))
        total = total + length(here, before)
        arc[j] = total
        return (*here, total)

    arc[0] = zero
    top = lax.fori_loop(
        1, ROWS, inner, (*(grid[c, 1] for c in range(3)), zero), unroll=4
    )

    beyond = jnp.where((rad == half - 1) | (rad == half), 1, 0)
    higher = jnp.where(tan > 0, 1, 0) + jnp.where(tan == ntan - 1, 1, 0)
    pl.semaphore_wait(barrier, 2 + half - 1 + beyond + higher)

    row = (row_s, row_r)
    to_above = [
        send(coords.at[0, :, ROWS - 1], grid.at[:, 0], row, 0, above),
        send(state.at[0, :, pl.ds(ROWS - 2, 2)], flow.at[:, pl.ds(0, 2)], row, 1, above),
    ]
    to_below = [
        send(coords.at[0, :, 0], grid.at[:, ROWS + 1], row, 2, below),
        send(state.at[0, :, pl.ds(0, 2)], flow.at[:, pl.ds(ROWS + 2, 2)], row, 3, below),
    ]
    walls = [
        send(coords.at[0, pl.ds(1, 2), 0], wall, (wall_s, wall_r), k, device)
        for k, device in enumerate([across] + peers)
    ]
    passed = [send(wall, wall, (wall_s, wall_r), k + 1, device) for k, device in enumerate(peers)]
    count = ROWS // CHUNKS
    bulk = [
        send(
            state.at[0, :, pl.ds(k * count, count)],
            state_in.at[:, pl.ds(k * count, count)],
            (bulk_s, bulk_r), k, partner,
        )
        for k in range(CHUNKS)
    ]

    @pl.when(rad < nrad - 1)
    def _():
        to_above[0].start()

    @pl.when(rad > 0)
    def _():
        to_below[0].start()

    @pl.when(first)
    def _():
        for copy in walls:
            copy.start()

    @pl.when(rad < nrad - 1)
    def _():
        to_above[1].start()

    @pl.when(rad > 0)
    def _():
        to_below[1].start()

    for copy in bulk:
        copy.start()

    @pl.when(tan > 0)
    def _():
        pl.semaphore_signal(ready_right, inc=1, device_id=left, device_id_type=MESH)

    @pl.when(tan == ntan - 1)
    def _():
        pl.semaphore_signal(ready_left, inc=1, device_id=right, device_id_type=MESH)

    loads[1].wait()

    def over_tan(j, packed):
        here = [flow[c, j + 2] for c in range(5)]
        m2, m1, p1, p2 = ([pltpu.roll(w, k, 1) for w in here] for k in (2, 1, 127, 126))
        odd, even = jst(m2, m1, here, p1, p2)
        for c in range(5):
            odd_t[c, j] = odd[c]
            even_t[c, j] = even[c]
        mine, shift = row_of == j, (4 * j + 2) % 128
        tight = [
            jnp.where(mine, pltpu.roll(here[c], shift, 1), packed[c]) for c in range(5)
        ]
        wide = [
            jnp.where(mine, pltpu.roll(jnp.where(lane < 64, p2[c], m2[c]), shift, 1), packed[c + 5])
            for c in range(5)
        ]
        return (*tight, *wide)

    packed = each_row(over_tan, (zero,) * 10)
    tight, wide = packed[:5], packed[5:]
    for c in range(5):
        edge_out[c] = tight[c]

    @pl.when(rad > 0)
    def _():
        to_above[0].wait_recv()

    @pl.when(first)
    def _():
        for c in range(3):
            grid[c, 0] = grid[c, 1]

    step_in = length([grid[c, 1] for c in range(3)], [grid[c, 0] for c in range(3)])
    line = step_in + top[3]
    sums[place] = line
    sum_sends = [
        send(sums.at[place], sums.at[place], (sum_s, sum_r), k, device)
        for k, device in enumerate(peers)
    ]
    for copy in sum_sends:
        copy.start()

    @pl.when(rad == half)
    def _():
        walls[0].wait_recv()
        for copy in passed:
            copy.start()

    for load in loads[3:]:
        load.wait()
    own_id = jnp.where(inst == 0, ids_s[0], ids_s[1])
    other_id = jnp.where(inst == 0, ids_s[1], ids_s[0])
    offset_id = own_id - other_id
    turn = 2.0 * jnp.pi / NINST
    own_phase = turn * own_id.astype(jnp.float32) + motion_s[1]
    other_phase = turn * other_id.astype(jnp.float32) + motion_s[1]
    angle = (jnp.pi / NINST) * offset_id.astype(jnp.float32)
    angles = jnp.where(span == 0, own_phase, jnp.where(span == 1, other_phase, angle))
    sines, cosines = jnp.sin(angles), jnp.cos(angles)

    def pick(values, k):
        return jnp.broadcast_to(values[k : k + 1], TILE)

    theta = motion_s[0] * pick(sines, 0)
    sin_theta, cos_theta = jnp.sin(theta), jnp.cos(theta)
    own_far = [heave_s[c] * pick(cosines, 0) for c in range(3)]
    other_far = [heave_s[c] * pick(cosines, 1) for c in range(3)]
    parity = 1.0 - 2.0 * lax.rem(offset_id + NINST, 2).astype(jnp.float32)
    coef = 0.5 * parity * pick(cosines, 2) / pick(sines, 2)

    for copy in sum_sends:
        copy.wait_recv()
    own_half, lower = zero, zero
    for k in range(half):
        part = sums[k]
        own_half = own_half + part
        lower = lower + jnp.where(k < place, part, 0.0)
    cross_out[...] = own_half
    one = (one_s, one_r)
    cross = send(cross_out, cross_in, one, 2, across)
    cross.start()

    @pl.when(rad > 0)
    def _():
        to_above[1].wait_recv()

    @pl.when(first)
    def _():
        flow[:, 0:2] = jnp.zeros((5, 2, *TILE), jnp.float32)

    @pl.when(rad < nrad - 1)
    def _():
        to_below[1].wait_recv()

    @pl.when(last)
    def _():
        flow[:, ROWS + 2 : ROWS + 4] = jnp.zeros((5, 2, *TILE), jnp.float32)

    def over_rad(j, carry):
        odd, even = jst(*([flow[c, j + k] for c in range(5)] for k in range(5)))
        for c in range(5):
            odd_r[c, j] = odd[c]
            even_r[c, j] = even[c]
        return carry

    lax.fori_loop(0, ROWS, over_rad, 0, unroll=2)

    @pl.when(first)
    def _():
        for c in range(2):
            wall[c] = grid[c + 1, 1]

    @pl.when((rad != 0) & (rad != half))
    def _():
        for k in range(half - 1):

            @pl.when(place == k + 1)
            def _():
                walls[k + 1].wait_recv()

    @pl.when(rad < nrad - 1)
    def _():
        to_below[0].wait_recv()

    @pl.when(last)
    def _():
        for c in range(3):
            grid[c, ROWS + 1] = grid[c, ROWS]

    step_out = length([grid[c, ROWS + 1] for c in range(3)], [grid[c, ROWS] for c in range(3)])
    wall_y, wall_z = wall[0], wall[1]
    own_wall = [
        zero,
        wall_y * cos_theta - wall_z * sin_theta - wall_y,
        wall_y * sin_theta + wall_z * cos_theta - wall_z,
    ]
    frac_out[ROWS] = own_wall[1]
    frac_out[ROWS + 1] = own_wall[2]

    cross.wait_recv()
    other_half = cross_in[...]
    inverse = 1.0 / (own_half + other_half)
    offset = lower + jnp.where(side == 1, other_half, 0.0)
    base = offset + step_in

    def displaced(frac):
        return [
            frac * own_far[0],
            (1.0 - frac) * own_wall[1] + frac * own_far[1],
            (1.0 - frac) * own_wall[2] + frac * own_far[2],
        ]

    def move(j, edge):
        frac = (base + arc[j]) * inverse
        frac_out[j] = frac
        mine, shift = row_of == j, (4 * j + 2) % 128
        out = []
        for c, d in enumerate(displaced(frac)):
            disp_out[c, j] = d
            point = grid[c, j + 1] + d
            moved[c, j + 1] = point
            out.append(jnp.where(mine, pltpu.roll(point, shift, 1), edge[c]))
        return tuple(out)

    edges = each_row(move, (zero,) * 3)

    def slab(src, dst, sems, k):
        size = ROWS // PARTS
        extra = src.shape[0] - ROWS if k == PARTS - 1 else 0
        part = pl.ds(k * size, size + extra)
        return send(src.at[part], dst.at[part], sems, k, partner)

    frac_sends = [slab(frac_out, frac_in, (frac_s, frac_r), k) for k in range(PARTS)]
    for copy in frac_sends:
        copy.start()
    for c in range(3):
        edge_out[5 + c] = edges[c]
    edge_sends = [
        send(edge_out, edge_left, one, 0, right),
        send(edge_out, edge_right, one, 1, left),
    ]

    @pl.when(tan < ntan - 1)
    def _():
        pl.semaphore_wait(ready_right, 1)

    edge_sends[0].start()

    @pl.when(tan == 0)
    def _():
        pl.semaphore_wait(ready_left, 1)

    edge_sends[1].start()

    for c, d in enumerate(displaced(offset * inverse)):
        moved[c, 0] = grid[c, 0] + d
    for c, d in enumerate(displaced((base + top[3] + step_out) * inverse)):
        moved[c, ROWS + 1] = grid[c, ROWS + 1] + d

    @pl.when(first)
    def _():
        for c in range(3):
            moved[c, 0] = moved[c, 1]

    @pl.when(last)
    def _():
        for c in range(3):
            moved[c, ROWS + 1] = moved[c, ROWS]

    at_low, at_high = span == 0, span == 7
    span_scale = jnp.where(at_low | at_high, 1.0, 0.5)

    def slopes(j, packed):
        outer = first if j == 0 else last if j == ROWS - 1 else False
        scale = jnp.where(outer, 1.0, 0.5)
        t, r, z = [], [], []
        for c in range(3):
            here = moved[c, j + 1]
            t.append((pltpu.roll(here, 127, 1) - pltpu.roll(here, 1, 1)) * 0.5)
            r.append((moved[c, j + 2] - moved[c, j]) * scale)
            over = jnp.where(at_high, here, pltpu.roll(here, 7, 0))
            under = jnp.where(at_low, here, pltpu.roll(here, 1, 0))
            z.append((over - under) * span_scale)
            e_t[c, j] = t[c]
            e_r[c, j] = r[c]
        face = [
            z[1] * r[2] - z[2] * r[1],
            z[2] * r[0] - z[0] * r[2],
            z[0] * r[1] - z[1] * r[0],
        ]
        vol_out[j] = t[0] * face[0] + t[1] * face[1] + t[2] * face[2]
        mine, shift = row_of == j, (4 * j + 2) % 128
        return tuple(
            jnp.where(mine, pltpu.roll(face[c], shift, 1), packed[c]) for c in range(3)
        )

    face = each_row(slopes, (zero,) * 3)
    vol_sends = [slab(vol_out, vol_in, (vol_s, vol_r), k) for k in range(PARTS)]
    for copy in vol_sends:
        copy.start()

    for copy in edge_sends:
        copy.wait_recv()
    beside = [jnp.where(slot < 2, edge_left[c], edge_right[c]) for c in range(8)]
    rim = []
    for c in range(3):
        ahead = pltpu.roll(jnp.where(slot == 2, beside[5 + c], edges[c]), 127, 1)
        behind = pltpu.roll(jnp.where(slot == 1, beside[5 + c], edges[c]), 1, 1)
        rim.append((ahead - behind) * 0.5)
    rim_out[...] = rim[0] * face[0] + rim[1] * face[1] + rim[2] * face[2]
    rim_send = send(rim_out, rim_in, one, 3, partner)
    rim_send.start()
    m1, p1, m2, p2 = [], [], [], []
    for c in range(5):
        m2.append(jnp.where(slot < 2, wide[c], pltpu.roll(beside[c], 2, 1)))
        p2.append(jnp.where(slot < 2, pltpu.roll(beside[c], 126, 1), wide[c]))
        near = pltpu.roll(jnp.where(slot == 1, beside[c], tight[c]), 1, 1)
        m1.append(jnp.where(slot == 0, pltpu.roll(wide[c], 127, 1), near))
        near = pltpu.roll(jnp.where(slot == 2, beside[c], tight[c]), 127, 1)
        p1.append(jnp.where(slot == 3, pltpu.roll(wide[c], 1, 1), near))
    rim_odd, rim_even = jst(m2, m1, tight, p1, p2)

    loads[2].wait()
    for copy in frac_sends:
        copy.wait_recv()
    other_wall = [zero, frac_in[ROWS], frac_in[ROWS + 1]]
    start = [stream_s[c] - coef * other_wall[c] for c in range(3)]
    slope = [coef * (other_wall[c] - other_far[c]) for c in range(3)]
    outer_two = (lane < 2) | (lane > 125)
    outer_one = (lane == 0) | (lane == 127)

    def fluxes(j, carry):
        shift = (126 - 4 * j) % 128
        frac = frac_in[j]
        relative = [start[c] + frac * slope[c] for c in range(3)]
        tangent = [jnp.where(outer_one, pltpu.roll(rim[c], shift, 1), e_t[c, j]) for c in range(3)]
        speed_t = sum(relative[c] * tangent[c] for c in range(3))
        speed_r = sum(relative[c] * e_r[c, j] for c in range(3))
        size_t, size_r = jnp.abs(speed_t), jnp.abs(speed_r)
        for c in range(5):
            odd = jnp.where(outer_two, pltpu.roll(rim_odd[c], shift, 1), odd_t[c, j])
            even = jnp.where(outer_two, pltpu.roll(rim_even[c], shift, 1), even_t[c, j])
            over_t = speed_t * odd - size_t * even
            over_r = speed_r * odd_r[c, j] - size_r * even_r[c, j]
            res_out[c, j] = over_t + over_r + rest_v[c, j]
        return carry

    each_row(fluxes, 0)

    for copy in bulk + vol_sends + [rim_send]:
        copy.wait_recv()
    rim_vol = rim_in[...]

    def add(j, carry):
        shift = (126 - 4 * j) % 128
        weight = coef * jnp.where(outer_one, pltpu.roll(rim_vol, shift, 1), vol_in[j])
        for c in range(5):
            res_out[c, j] = res_out[c, j] + weight * state_in[c, j]
        return carry

    each_row(add, 0)

    @pl.when(rad < nrad - 1)
    def _():
        for copy in to_above:
            copy.wait_send()

    @pl.when(rad > 0)
    def _():
        for copy in to_below:
            copy.wait_send()

    @pl.when(first)
    def _():
        for copy in walls:
            copy.wait_send()

    @pl.when(rad == half)
    def _():
        for copy in passed:
            copy.wait_send()

    for copy in sum_sends + [cross, rim_send] + edge_sends + frac_sends + vol_sends + bulk:
        copy.wait_send()


def store_kernel(disp, res, disp_out, res_out, sems):
    copies = [
        pltpu.make_async_copy(disp, disp_out.at[0], sems.at[0]),
        pltpu.make_async_copy(res, res_out.at[0], sems.at[1]),
    ]
    for copy in copies:
        copy.start()
    for copy in copies:
        copy.wait()


def body(nrad, ntan, *args):
    half = nrad // 2
    f32 = jnp.float32
    vmem, hbm = pltpu.VMEM, pltpu.HBM

    def tiles(*lead):
        return pltpu.VMEM((*lead, *TILE), f32)

    dma = pltpu.SemaphoreType.DMA
    scratch = [
        tiles(3, ROWS + 2), tiles(5, ROWS + 4), tiles(5, ROWS), tiles(3, ROWS + 2), tiles(ROWS),
        tiles(ROWS + 2), tiles(ROWS + 2), tiles(3, ROWS), tiles(3, ROWS), tiles(ROWS), tiles(ROWS),
        tiles(5, ROWS), tiles(5, ROWS), tiles(5, ROWS), tiles(5, ROWS), tiles(5, ROWS),
        tiles(2), tiles(half), tiles(), tiles(), tiles(8), tiles(8), tiles(8), tiles(), tiles(),
        pltpu.SMEM((2,), jnp.int32), pltpu.SMEM((2,), f32), pltpu.SMEM((3,), f32), pltpu.SMEM((3,), f32),
        dma((7,)), dma((CHUNKS,)), dma((CHUNKS,)), dma((4,)), dma((4,)),
        dma((half,)), dma((half,)), dma((half - 1,)), dma((half - 1,)), dma((4,)), dma((4,)),
        dma((PARTS,)), dma((PARTS,)), dma((PARTS,)), dma((PARTS,)),
        pltpu.SemaphoreType.REGULAR, pltpu.SemaphoreType.REGULAR,
    ]
    disp, res = pl.pallas_call(
        functools.partial(step_kernel, nrad, ntan),
        out_shape=[
            jax.ShapeDtypeStruct((3, ROWS, *TILE), f32),
            jax.ShapeDtypeStruct((5, ROWS, *TILE), f32),
        ],
        in_specs=[pl.BlockSpec(memory_space=hbm)] * 7,
        out_specs=[pl.BlockSpec(memory_space=vmem)] * 2,
        scratch_shapes=scratch,
        name="deform_and_residual",
        compiler_params=pltpu.CompilerParams(
            collective_id=0, has_side_effects=True, vmem_limit_bytes=24 * 2**20
        ),
    )(*(pltpu.with_memory_space_constraint(arg, hbm) for arg in args))
    return pl.pallas_call(
        store_kernel,
        out_shape=[
            jax.ShapeDtypeStruct((1, 3, ROWS, *TILE), f32),
            jax.ShapeDtypeStruct((1, 5, ROWS, *TILE), f32),
        ],
        in_specs=[pl.BlockSpec(memory_space=vmem)] * 2,
        out_specs=[pl.BlockSpec(memory_space=hbm)] * 2,
        scratch_shapes=[dma((2,))],
        name="store_results",
    )(*(pltpu.with_memory_space_constraint(x, vmem) for x in (disp, res)))


def solution(mesh):
    split = P("inst", None, "rad", None, "tan")
    return jax.shard_map(
        functools.partial(body, mesh.shape["rad"], mesh.shape["tan"]),
        mesh=mesh,
        in_specs=(split, split, split, P(), P(), P(), P()),
        out_specs=(split, split),
        check_vma=False,
    )
```

```python
import functools

import jax
import jax.numpy as jnp
from jax import lax
from jax.experimental import pallas as pl
from jax.experimental.pallas import tpu as pltpu
from jax.sharding import PartitionSpec as P

NINST = 16
COEF_TWO = 0.1
COEF_FOUR = 0.05
MESH = pl.DeviceIdType.MESH
ROWS = 32
CHUNKS = 8
PARTS = 4
TILE = (8, 128)


def send(src, dst, sems, slot, device):
    return pltpu.make_async_remote_copy(
        src_ref=src,
        dst_ref=dst,
        send_sem=sems[0].at[slot],
        recv_sem=sems[1].at[slot],
        device_id=device,
        device_id_type=MESH,
    )


def length(a, b):
    d = [p - q for p, q in zip(a, b)]
    return jnp.sqrt(d[0] * d[0] + d[1] * d[1] + d[2] * d[2])


def each_row(body, carry):
    for j in range(ROWS):
        carry = body(j, carry)
    return carry


def jst(m2, m1, c, p1, p2):
    q_m, q_c, q_p = (1.0 + w[0] * w[0] for w in (m1, c, p1))
    outer = q_p + q_m
    sensor = COEF_TWO * jnp.abs(outer - 2.0 * q_c) / (outer + 2.0 * q_c)
    fourth = jnp.maximum(0.0, COEF_FOUR - sensor)
    near = sensor + 4.0 * fourth
    mid = 2.0 * sensor + 6.0 * fourth
    odd = [0.5 * (p1[k] - m1[k]) for k in range(5)]
    even = [near * (p1[k] + m1[k]) - mid * c[k] - fourth * (p2[k] + m2[k]) for k in range(5)]
    return odd, even


def step_kernel(
    nrad, ntan,
    coords, state, rest, ids, motion, heave, stream,
    disp_out, res_out,
    grid, flow, rest_v, moved, arc, frac_out, frac_in, e_t, e_r, vol_out, vol_in, state_in,
    odd_t, even_t, odd_r, even_r,
    wall, sums, far_out, far_in, far_prior, edge_out, edge_left, edge_right, rim_out, rim_in,
    ids_s, motion_s, heave_s, stream_s,
    local, bulk_s, bulk_r, row_s, row_r, wall_s, wall_r, sum_s, sum_r, one_s, one_r,
    frac_s, frac_r, vol_s, vol_r, ready_right, ready_left,
):
    rad, tan, inst = lax.axis_index("rad"), lax.axis_index("tan"), lax.axis_index("inst")
    half = nrad // 2
    place, side = lax.rem(rad, half), rad // half
    first, last = rad == 0, rad == nrad - 1
    partner = {"inst": 1 - inst}
    left = {"tan": lax.rem(tan + ntan - 1, ntan)}
    right = {"tan": lax.rem(tan + 1, ntan)}
    above = {"rad": lax.rem(rad + 1, nrad)}
    below = {"rad": lax.rem(rad + nrad - 1, nrad)}
    across = {"rad": lax.rem(rad + half, nrad)}
    peers = [{"rad": side * half + lax.rem(place + k, half)} for k in range(1, half)]

    loads = [
        pltpu.make_async_copy(coords.at[0], grid.at[:, pl.ds(1, ROWS)], local.at[0]),
        pltpu.make_async_copy(state.at[0], flow.at[:, pl.ds(2, ROWS)], local.at[1]),
        pltpu.make_async_copy(rest.at[0], rest_v, local.at[2]),
        pltpu.make_async_copy(ids, ids_s, local.at[3]),
        pltpu.make_async_copy(motion, motion_s, local.at[4]),
        pltpu.make_async_copy(heave, heave_s, local.at[5]),
        pltpu.make_async_copy(stream, stream_s, local.at[6]),
    ]
    barrier = pltpu.get_barrier_semaphore()

    def greet(device):
        pl.semaphore_signal(barrier, inc=1, device_id=device, device_id_type=MESH)

    for device in [partner, across] + peers:
        greet(device)
    pl.when(rad == half - 1)(lambda: greet(above))
    pl.when(rad == half)(lambda: greet(below))
    pl.when(tan < ntan - 1)(lambda: greet(right))
    pl.when(tan == 0)(lambda: greet(left))
    for load in loads:
        load.start()

    lane = lax.broadcasted_iota(jnp.int32, TILE, 1)
    span = lax.broadcasted_iota(jnp.int32, TILE, 0)
    zero = jnp.zeros(TILE, jnp.float32)
    row_of, slot = lane // 4, lax.rem(lane, 4)

    loads[0].wait()

    def inner(j, carry):
        before, total = carry[:3], carry[3]
        here = tuple(grid[c, j + 1] for c in range(3))
        total = total + length(here, before)
        arc[j] = total
        return (*here, total)

    arc[0] = zero
    top = lax.fori_loop(
        1, ROWS, inner, (*(grid[c, 1] for c in range(3)), zero), unroll=4
    )

    beyond = jnp.where((rad == half - 1) | (rad == half), 1, 0)
    higher = jnp.where(tan > 0, 1, 0) + jnp.where(tan == ntan - 1, 1, 0)
    pl.semaphore_wait(barrier, 2 + half - 1 + beyond + higher)

    for c in range(3):
        far_out[c] = grid[c, 1]
        far_out[3 + c] = grid[c, ROWS]
    far_out[6] = top[3]
    one = (one_s, one_r)
    far = send(far_out, far_in, one, 2, across)
    far_last = send(far_in.at[pl.ds(3, 3)], far_prior, one, 4, above)
    row = (row_s, row_r)
    to_above = [
        send(coords.at[0, :, ROWS - 1], grid.at[:, 0], row, 0, above),
        send(state.at[0, :, pl.ds(ROWS - 2, 2)], flow.at[:, pl.ds(0, 2)], row, 1, above),
    ]
    to_below = [
        send(coords.at[0, :, 0], grid.at[:, ROWS + 1], row, 2, below),
        send(state.at[0, :, pl.ds(0, 2)], flow.at[:, pl.ds(ROWS + 2, 2)], row, 3, below),
    ]
    walls = [
        send(coords.at[0, pl.ds(1, 2), 0], wall, (wall_s, wall_r), k, device)
        for k, device in enumerate([across] + peers)
    ]
    passed = [send(wall, wall, (wall_s, wall_r), k + 1, device) for k, device in enumerate(peers)]
    count = ROWS // CHUNKS
    bulk = [
        send(
            state.at[0, :, pl.ds(k * count, count)],
            state_in.at[:, pl.ds(k * count, count)],
            (bulk_s, bulk_r), k, partner,
        )
        for k in range(CHUNKS)
    ]

    far.start()

    @pl.when(rad < nrad - 1)
    def _():
        to_above[0].start()

    @pl.when(rad > 0)
    def _():
        to_below[0].start()

    @pl.when(first)
    def _():
        for copy in walls:
            copy.start()

    @pl.when(rad < nrad - 1)
    def _():
        to_above[1].start()

    @pl.when(rad > 0)
    def _():
        to_below[1].start()

    for copy in bulk:
        copy.start()

    @pl.when(tan > 0)
    def _():
        pl.semaphore_signal(ready_right, inc=1, device_id=left, device_id_type=MESH)

    @pl.when(tan == ntan - 1)
    def _():
        pl.semaphore_signal(ready_left, inc=1, device_id=right, device_id_type=MESH)

    far.wait_recv()

    @pl.when(place < half - 1)
    def _():
        far_last.start()

    @pl.when(rad > 0)
    def _():
        to_above[0].wait_recv()

    @pl.when(first)
    def _():
        for c in range(3):
            grid[c, 0] = grid[c, 1]

    @pl.when(rad < nrad - 1)
    def _():
        to_below[0].wait_recv()

    @pl.when(last)
    def _():
        for c in range(3):
            grid[c, ROWS + 1] = grid[c, ROWS]

    step_in = length([grid[c, 1] for c in range(3)], [grid[c, 0] for c in range(3)])
    step_out = length([grid[c, ROWS + 1] for c in range(3)], [grid[c, ROWS] for c in range(3)])

    @pl.when(place > 0)
    def _():
        far_last.wait_recv()

    @pl.when(place == 0)
    def _():
        for c in range(3):
            far_prior[c] = far_in[c]

    far_step = length([far_in[c] for c in range(3)], [far_prior[c] for c in range(3)])
    sums[place, 0] = step_in + top[3]
    sums[place, 1] = far_in[6] + far_step + jnp.where(rad == half - 1, step_out, 0.0)
    sum_sends = [
        send(sums.at[place], sums.at[place], (sum_s, sum_r), k, device)
        for k, device in enumerate(peers)
    ]
    for copy in sum_sends:
        copy.start()

    @pl.when(rad == half)
    def _():
        walls[0].wait_recv()
        for copy in passed:
            copy.start()

    loads[1].wait()

    def over_tan(j, packed):
        here = [flow[c, j + 2] for c in range(5)]
        m2, m1, p1, p2 = ([pltpu.roll(w, k, 1) for w in here] for k in (2, 1, 127, 126))
        odd, even = jst(m2, m1, here, p1, p2)
        for c in range(5):
            odd_t[c, j] = odd[c]
            even_t[c, j] = even[c]
        mine, shift = row_of == j, (4 * j + 2) % 128
        tight = [
            jnp.where(mine, pltpu.roll(here[c], shift, 1), packed[c]) for c in range(5)
        ]
        wide = [
            jnp.where(mine, pltpu.roll(jnp.where(lane < 64, p2[c], m2[c]), shift, 1), packed[c + 5])
            for c in range(5)
        ]
        return (*tight, *wide)

    packed = each_row(over_tan, (zero,) * 10)
    tight, wide = packed[:5], packed[5:]
    for c in range(5):
        edge_out[c] = tight[c]

    for load in loads[3:]:
        load.wait()
    own_id = jnp.where(inst == 0, ids_s[0], ids_s[1])
    other_id = jnp.where(inst == 0, ids_s[1], ids_s[0])
    offset_id = own_id - other_id
    turn = 2.0 * jnp.pi / NINST
    own_phase = turn * own_id.astype(jnp.float32) + motion_s[1]
    other_phase = turn * other_id.astype(jnp.float32) + motion_s[1]
    angle = (jnp.pi / NINST) * offset_id.astype(jnp.float32)
    angles = jnp.where(span == 0, own_phase, jnp.where(span == 1, other_phase, angle))
    sines, cosines = jnp.sin(angles), jnp.cos(angles)

    def pick(values, k):
        return jnp.broadcast_to(values[k : k + 1], TILE)

    theta = motion_s[0] * pick(sines, 0)
    sin_theta, cos_theta = jnp.sin(theta), jnp.cos(theta)
    own_far = [heave_s[c] * pick(cosines, 0) for c in range(3)]
    other_far = [heave_s[c] * pick(cosines, 1) for c in range(3)]
    parity = 1.0 - 2.0 * lax.rem(offset_id + NINST, 2).astype(jnp.float32)
    coef = 0.5 * parity * pick(cosines, 2) / pick(sines, 2)

    for copy in sum_sends:
        copy.wait_recv()
    own_half, other_half, lower = zero, zero, zero
    for k in range(half):
        own_half = own_half + sums[k, 0]
        other_half = other_half + sums[k, 1]
        lower = lower + jnp.where(k < place, sums[k, 0], 0.0)

    @pl.when(first)
    def _():
        for c in range(2):
            wall[c] = grid[c + 1, 1]

    @pl.when((rad != 0) & (rad != half))
    def _():
        for k in range(half - 1):

            @pl.when(place == k + 1)
            def _():
                walls[k + 1].wait_recv()

    wall_y, wall_z = wall[0], wall[1]
    own_wall = [
        zero,
        wall_y * cos_theta - wall_z * sin_theta - wall_y,
        wall_y * sin_theta + wall_z * cos_theta - wall_z,
    ]
    frac_out[ROWS] = own_wall[1]
    frac_out[ROWS + 1] = own_wall[2]

    inverse = 1.0 / (own_half + other_half)
    offset = lower + jnp.where(side == 1, other_half, 0.0)
    base = offset + step_in

    def displaced(frac):
        return [
            frac * own_far[0],
            (1.0 - frac) * own_wall[1] + frac * own_far[1],
            (1.0 - frac) * own_wall[2] + frac * own_far[2],
        ]

    def move(j, edge):
        frac = (base + arc[j]) * inverse
        frac_out[j] = frac
        mine, shift = row_of == j, (4 * j + 2) % 128
        out = []
        for c, d in enumerate(displaced(frac)):
            disp_out[c, j] = d
            point = grid[c, j + 1] + d
            moved[c, j + 1] = point
            out.append(jnp.where(mine, pltpu.roll(point, shift, 1), edge[c]))
        return tuple(out)

    edges = each_row(move, (zero,) * 3)

    def slab(src, dst, sems, k):
        size = ROWS // PARTS
        extra = src.shape[0] - ROWS if k == PARTS - 1 else 0
        part = pl.ds(k * size, size + extra)
        return send(src.at[part], dst.at[part], sems, k, partner)

    frac_sends = [slab(frac_out, frac_in, (frac_s, frac_r), k) for k in range(PARTS)]
    for copy in frac_sends:
        copy.start()
    for c in range(3):
        edge_out[5 + c] = edges[c]
    edge_sends = [
        send(edge_out, edge_left, one, 0, right),
        send(edge_out, edge_right, one, 1, left),
    ]

    @pl.when(tan < ntan - 1)
    def _():
        pl.semaphore_wait(ready_right, 1)

    edge_sends[0].start()

    @pl.when(tan == 0)
    def _():
        pl.semaphore_wait(ready_left, 1)

    edge_sends[1].start()

    for c, d in enumerate(displaced(offset * inverse)):
        moved[c, 0] = grid[c, 0] + d
    for c, d in enumerate(displaced((base + top[3] + step_out) * inverse)):
        moved[c, ROWS + 1] = grid[c, ROWS + 1] + d

    @pl.when(first)
    def _():
        for c in range(3):
            moved[c, 0] = moved[c, 1]

    @pl.when(last)
    def _():
        for c in range(3):
            moved[c, ROWS + 1] = moved[c, ROWS]

    at_low, at_high = span == 0, span == 7
    span_scale = jnp.where(at_low | at_high, 1.0, 0.5)

    def slopes(j, packed):
        outer = first if j == 0 else last if j == ROWS - 1 else False
        scale = jnp.where(outer, 1.0, 0.5)
        t, r, z = [], [], []
        for c in range(3):
            here = moved[c, j + 1]
            t.append((pltpu.roll(here, 127, 1) - pltpu.roll(here, 1, 1)) * 0.5)
            r.append((moved[c, j + 2] - moved[c, j]) * scale)
            over = jnp.where(at_high, here, pltpu.roll(here, 7, 0))
            under = jnp.where(at_low, here, pltpu.roll(here, 1, 0))
            z.append((over - under) * span_scale)
            e_t[c, j] = t[c]
            e_r[c, j] = r[c]
        face = [
            z[1] * r[2] - z[2] * r[1],
            z[2] * r[0] - z[0] * r[2],
            z[0] * r[1] - z[1] * r[0],
        ]
        vol_out[j] = t[0] * face[0] + t[1] * face[1] + t[2] * face[2]
        mine, shift = row_of == j, (4 * j + 2) % 128
        return tuple(
            jnp.where(mine, pltpu.roll(face[c], shift, 1), packed[c]) for c in range(3)
        )

    face = each_row(slopes, (zero,) * 3)
    vol_sends = [slab(vol_out, vol_in, (vol_s, vol_r), k) for k in range(PARTS)]
    for copy in vol_sends:
        copy.start()

    @pl.when(rad > 0)
    def _():
        to_above[1].wait_recv()

    @pl.when(first)
    def _():
        flow[:, 0:2] = jnp.zeros((5, 2, *TILE), jnp.float32)

    @pl.when(rad < nrad - 1)
    def _():
        to_below[1].wait_recv()

    @pl.when(last)
    def _():
        flow[:, ROWS + 2 : ROWS + 4] = jnp.zeros((5, 2, *TILE), jnp.float32)

    def over_rad(j, carry):
        odd, even = jst(*([flow[c, j + k] for c in range(5)] for k in range(5)))
        for c in range(5):
            odd_r[c, j] = odd[c]
            even_r[c, j] = even[c]
        return carry

    lax.fori_loop(0, ROWS, over_rad, 0, unroll=2)

    for copy in edge_sends:
        copy.wait_recv()
    beside = [jnp.where(slot < 2, edge_left[c], edge_right[c]) for c in range(8)]
    rim = []
    for c in range(3):
        ahead = pltpu.roll(jnp.where(slot == 2, beside[5 + c], edges[c]), 127, 1)
        behind = pltpu.roll(jnp.where(slot == 1, beside[5 + c], edges[c]), 1, 1)
        rim.append((ahead - behind) * 0.5)
    rim_out[...] = rim[0] * face[0] + rim[1] * face[1] + rim[2] * face[2]
    rim_send = send(rim_out, rim_in, one, 3, partner)
    rim_send.start()
    m1, p1, m2, p2 = [], [], [], []
    for c in range(5):
        m2.append(jnp.where(slot < 2, wide[c], pltpu.roll(beside[c], 2, 1)))
        p2.append(jnp.where(slot < 2, pltpu.roll(beside[c], 126, 1), wide[c]))
        near = pltpu.roll(jnp.where(slot == 1, beside[c], tight[c]), 1, 1)
        m1.append(jnp.where(slot == 0, pltpu.roll(wide[c], 127, 1), near))
        near = pltpu.roll(jnp.where(slot == 2, beside[c], tight[c]), 127, 1)
        p1.append(jnp.where(slot == 3, pltpu.roll(wide[c], 1, 1), near))
    rim_odd, rim_even = jst(m2, m1, tight, p1, p2)

    loads[2].wait()
    for copy in frac_sends:
        copy.wait_recv()
    other_wall = [zero, frac_in[ROWS], frac_in[ROWS + 1]]
    start = [stream_s[c] - coef * other_wall[c] for c in range(3)]
    slope = [coef * (other_wall[c] - other_far[c]) for c in range(3)]
    outer_two = (lane < 2) | (lane > 125)
    outer_one = (lane == 0) | (lane == 127)

    def fluxes(j, carry):
        shift = (126 - 4 * j) % 128
        frac = frac_in[j]
        relative = [start[c] + frac * slope[c] for c in range(3)]
        tangent = [jnp.where(outer_one, pltpu.roll(rim[c], shift, 1), e_t[c, j]) for c in range(3)]
        speed_t = sum(relative[c] * tangent[c] for c in range(3))
        speed_r = sum(relative[c] * e_r[c, j] for c in range(3))
        size_t, size_r = jnp.abs(speed_t), jnp.abs(speed_r)
        for c in range(5):
            odd = jnp.where(outer_two, pltpu.roll(rim_odd[c], shift, 1), odd_t[c, j])
            even = jnp.where(outer_two, pltpu.roll(rim_even[c], shift, 1), even_t[c, j])
            over_t = speed_t * odd - size_t * even
            over_r = speed_r * odd_r[c, j] - size_r * even_r[c, j]
            res_out[c, j] = over_t + over_r + rest_v[c, j]
        return carry

    each_row(fluxes, 0)

    rim_send.wait_recv()
    rim_vol = rim_in[...]
    for k in range(PARTS):
        for copy in bulk[k * CHUNKS // PARTS : (k + 1) * CHUNKS // PARTS] + [vol_sends[k]]:
            copy.wait_recv()
        for j in range(k * ROWS // PARTS, (k + 1) * ROWS // PARTS):
            shift = (126 - 4 * j) % 128
            weight = coef * jnp.where(outer_one, pltpu.roll(rim_vol, shift, 1), vol_in[j])
            for c in range(5):
                res_out[c, j] = res_out[c, j] + weight * state_in[c, j]

    @pl.when(rad < nrad - 1)
    def _():
        for copy in to_above:
            copy.wait_send()

    @pl.when(rad > 0)
    def _():
        for copy in to_below:
            copy.wait_send()

    @pl.when(first)
    def _():
        for copy in walls:
            copy.wait_send()

    @pl.when(rad == half)
    def _():
        for copy in passed:
            copy.wait_send()

    @pl.when(place < half - 1)
    def _():
        far_last.wait_send()

    for copy in sum_sends + [far, rim_send] + edge_sends + frac_sends + vol_sends + bulk:
        copy.wait_send()


def store_kernel(disp, res, disp_out, res_out, sems):
    copies = [
        pltpu.make_async_copy(disp, disp_out.at[0], sems.at[0]),
        pltpu.make_async_copy(res, res_out.at[0], sems.at[1]),
    ]
    for copy in copies:
        copy.start()
    for copy in copies:
        copy.wait()


def body(nrad, ntan, *args):
    half = nrad // 2
    f32 = jnp.float32
    vmem, hbm = pltpu.VMEM, pltpu.HBM

    def tiles(*lead):
        return pltpu.VMEM((*lead, *TILE), f32)

    dma = pltpu.SemaphoreType.DMA
    scratch = [
        tiles(3, ROWS + 2), tiles(5, ROWS + 4), tiles(5, ROWS), tiles(3, ROWS + 2), tiles(ROWS),
        tiles(ROWS + 2), tiles(ROWS + 2), tiles(3, ROWS), tiles(3, ROWS), tiles(ROWS), tiles(ROWS),
        tiles(5, ROWS), tiles(5, ROWS), tiles(5, ROWS), tiles(5, ROWS), tiles(5, ROWS),
        tiles(2), tiles(half, 2), tiles(7), tiles(7), tiles(3), tiles(8), tiles(8), tiles(8), tiles(), tiles(),
        pltpu.SMEM((2,), jnp.int32), pltpu.SMEM((2,), f32), pltpu.SMEM((3,), f32), pltpu.SMEM((3,), f32),
        dma((7,)), dma((CHUNKS,)), dma((CHUNKS,)), dma((4,)), dma((4,)),
        dma((half,)), dma((half,)), dma((half - 1,)), dma((half - 1,)), dma((5,)), dma((5,)),
        dma((PARTS,)), dma((PARTS,)), dma((PARTS,)), dma((PARTS,)),
        pltpu.SemaphoreType.REGULAR, pltpu.SemaphoreType.REGULAR,
    ]
    disp, res = pl.pallas_call(
        functools.partial(step_kernel, nrad, ntan),
        out_shape=[
            jax.ShapeDtypeStruct((3, ROWS, *TILE), f32),
            jax.ShapeDtypeStruct((5, ROWS, *TILE), f32),
        ],
        in_specs=[pl.BlockSpec(memory_space=hbm)] * 7,
        out_specs=[pl.BlockSpec(memory_space=vmem)] * 2,
        scratch_shapes=scratch,
        name="deform_and_residual",
        compiler_params=pltpu.CompilerParams(
            collective_id=0, has_side_effects=True, vmem_limit_bytes=24 * 2**20
        ),
    )(*(pltpu.with_memory_space_constraint(arg, hbm) for arg in args))
    return pl.pallas_call(
        store_kernel,
        out_shape=[
            jax.ShapeDtypeStruct((1, 3, ROWS, *TILE), f32),
            jax.ShapeDtypeStruct((1, 5, ROWS, *TILE), f32),
        ],
        in_specs=[pl.BlockSpec(memory_space=vmem)] * 2,
        out_specs=[pl.BlockSpec(memory_space=hbm)] * 2,
        scratch_shapes=[dma((2,))],
        name="store_results",
    )(*(pltpu.with_memory_space_constraint(x, vmem) for x in (disp, res)))


def solution(mesh):
    split = P("inst", None, "rad", None, "tan")
    return jax.shard_map(
        functools.partial(body, mesh.shape["rad"], mesh.shape["tan"]),
        mesh=mesh,
        in_specs=(split, split, split, P(), P(), P(), P()),
        out_specs=(split, split),
        check_vma=False,
    )
```

```python
import functools

import jax
import jax.numpy as jnp
from jax import lax
from jax.experimental import pallas as pl
from jax.experimental.pallas import tpu as pltpu
from jax.sharding import PartitionSpec as P

NINST = 16
COEF_TWO = 0.1
COEF_FOUR = 0.05
MESH = pl.DeviceIdType.MESH
ROWS = 32
RAW = 24
CUTS = (0, 2, 8, 14, 20, RAW)
AHEAD = 3
PARTS = 4
TILE = (8, 128)


def send(src, dst, sems, slot, device):
    return pltpu.make_async_remote_copy(
        src_ref=src,
        dst_ref=dst,
        send_sem=sems[0].at[slot],
        recv_sem=sems[1].at[slot],
        device_id=device,
        device_id_type=MESH,
    )


def length(a, b):
    d = [p - q for p, q in zip(a, b)]
    return jnp.sqrt(d[0] * d[0] + d[1] * d[1] + d[2] * d[2])


def each_row(body, carry):
    for j in range(ROWS):
        carry = body(j, carry)
    return carry


def jst(m2, m1, c, p1, p2):
    q_m, q_c, q_p = (1.0 + w[0] * w[0] for w in (m1, c, p1))
    outer = q_p + q_m
    sensor = COEF_TWO * jnp.abs(outer - 2.0 * q_c) / (outer + 2.0 * q_c)
    fourth = jnp.maximum(0.0, COEF_FOUR - sensor)
    near = sensor + 4.0 * fourth
    mid = 2.0 * sensor + 6.0 * fourth
    odd = [0.5 * (p1[k] - m1[k]) for k in range(5)]
    even = [near * (p1[k] + m1[k]) - mid * c[k] - fourth * (p2[k] + m2[k]) for k in range(5)]
    return odd, even


def step_kernel(
    nrad, ntan,
    coords, state, rest, ids, motion, heave, stream,
    disp_out, res_out,
    grid, flow, rest_v, moved, arc, frac_out, frac_in, e_t, e_r, vol_out, vol_in, product_out, state_in,
    odd_t, even_t, odd_r, even_r,
    wall, sums, far_out, far_in, far_prior, edge_out, edge_left, edge_right, rim_out, rim_in,
    ids_s, motion_s, heave_s, stream_s,
    local, bulk_s, bulk_r, row_s, row_r, wall_s, wall_r, sum_s, sum_r, one_s, one_r,
    frac_s, frac_r, vol_s, vol_r, ready_rad, ready_next, ready_right, ready_left,
):
    rad, tan, inst = lax.axis_index("rad"), lax.axis_index("tan"), lax.axis_index("inst")
    half = nrad // 2
    place, side = lax.rem(rad, half), rad // half
    first, last = rad == 0, rad == nrad - 1
    partner = {"inst": 1 - inst}
    left = {"tan": lax.rem(tan + ntan - 1, ntan)}
    right = {"tan": lax.rem(tan + 1, ntan)}
    above = {"rad": lax.rem(rad + 1, nrad)}
    below = {"rad": lax.rem(rad + nrad - 1, nrad)}
    across = {"rad": lax.rem(rad + half, nrad)}
    peers = [{"rad": side * half + lax.rem(place + k, half)} for k in range(1, half)]

    loads = [
        pltpu.make_async_copy(coords.at[0], grid.at[:, pl.ds(1, ROWS)], local.at[0]),
        pltpu.make_async_copy(state.at[0], flow.at[:, pl.ds(2, ROWS)], local.at[1]),
        pltpu.make_async_copy(rest.at[0], rest_v, local.at[2]),
        pltpu.make_async_copy(ids, ids_s, local.at[3]),
        pltpu.make_async_copy(motion, motion_s, local.at[4]),
        pltpu.make_async_copy(heave, heave_s, local.at[5]),
        pltpu.make_async_copy(stream, stream_s, local.at[6]),
    ]
    barrier = pltpu.get_barrier_semaphore()
    turned = tan == 0

    def signal(semaphore, device, condition=None):
        def run():
            pl.semaphore_signal(semaphore, inc=1, device_id=device, device_id_type=MESH)

        run() if condition is None else pl.when(condition)(run)

    signal(barrier, partner)
    signal(barrier, across)
    for k, device in enumerate(peers):
        lower = place + k + 1 >= half
        signal(barrier, device, (lower & turned) | jnp.logical_not(lower | turned))
    signal(barrier, below, rad == half)
    signal(barrier, right, tan < ntan - 1)
    signal(barrier, left, turned)
    for load in loads:
        load.start()

    lane = lax.broadcasted_iota(jnp.int32, TILE, 1)
    span = lax.broadcasted_iota(jnp.int32, TILE, 0)
    zero = jnp.zeros(TILE, jnp.float32)
    row_of, slot = lane // 4, lax.rem(lane, 4)

    awaited = jnp.where(turned, half - 1 - place, place)
    higher = jnp.where(tan > 0, 1, 0) + jnp.where(tan == ntan - 1, 1, 0)
    pl.semaphore_wait(barrier, 2 + awaited + jnp.where(rad == half - 1, 1, 0) + higher)
    for k, device in enumerate(peers):
        lower = place + k + 1 >= half
        signal(ready_rad, device, (lower & jnp.logical_not(turned)) | (turned & jnp.logical_not(lower)))
    signal(ready_next, above, rad == half - 1)
    signal(ready_right, left, tan > 0)
    signal(ready_left, right, tan == ntan - 1)

    one = (one_s, one_r)
    far = send(far_out, far_in, one, 2, across)
    far_last = send(far_in.at[pl.ds(3, 3)], far_prior, one, 4, above)
    near_last = send(coords.at[0, :, ROWS - 1], far_prior, one, 4, peers[0])
    row = (row_s, row_r)
    to_above = [
        send(coords.at[0, :, ROWS - 1], grid.at[:, 0], row, 0, above),
        send(state.at[0, :, pl.ds(ROWS - 2, 2)], flow.at[:, pl.ds(0, 2)], row, 1, above),
    ]
    to_below = [
        send(coords.at[0, :, 0], grid.at[:, ROWS + 1], row, 2, below),
        send(state.at[0, :, pl.ds(0, 2)], flow.at[:, pl.ds(ROWS + 2, 2)], row, 3, below),
    ]
    far_first = send(far_in.at[pl.ds(0, 3)], grid.at[:, ROWS + 1], row, 2, peers[-1])
    walls = [
        send(coords.at[0, pl.ds(1, 2), 0], wall, (wall_s, wall_r), k, device)
        for k, device in enumerate([across] + peers)
    ]
    passed = [send(wall, wall, (wall_s, wall_r), k + 1, device) for k, device in enumerate(peers)]
    bulk = [
        send(
            state.at[0, :, pl.ds(low, high - low)],
            state_in.at[:, pl.ds(low, high - low)],
            (bulk_s, bulk_r), k, partner,
        )
        for k, (low, high) in enumerate(zip(CUTS, CUTS[1:]))
    ]

    pl.when(turned & (place < half - 1))(to_above[0].start)
    bulk[0].start()
    pl.when(rad == half - 1)(to_above[0].start)
    pl.when(first)(walls[0].start)

    loads[0].wait()

    def inner(j, carry):
        before, total = carry[:3], carry[3]
        here = tuple(grid[c, j + 1] for c in range(3))
        total = total + length(here, before)
        arc[j] = total
        return (*here, total)

    arc[0] = zero
    top = lax.fori_loop(
        1, ROWS, inner, (*(grid[c, 1] for c in range(3)), zero), unroll=4
    )

    for c in range(3):
        far_out[c] = grid[c, 1]
        far_out[3 + c] = grid[c, ROWS]
    far_out[6] = top[3]
    far.start()
    pl.when(rad == half - 1)(to_above[1].start)
    for copy in bulk[1:AHEAD]:
        copy.start()

    @pl.when(turned)
    def _():
        for copy in bulk[AHEAD:]:
            copy.start()

    pl.when(awaited < half - 1)(
        lambda: pl.semaphore_wait(ready_rad, half - 1 - awaited)
    )

    pl.when((place < half - 1) & jnp.logical_not(turned))(to_above[0].start)
    pl.when(place < half - 1)(to_above[1].start)
    pl.when(rad == half - 1)(near_last.start)

    @pl.when(first)
    def _():
        for copy in walls[1:]:
            copy.start()

    @pl.when(place > 0)
    def _():
        for copy in to_below:
            copy.start()

    far.wait_recv()
    pl.when(place < half - 1)(far_last.start)
    pl.when(first)(far_first.start)

    @pl.when(rad == half)
    def _():
        pl.semaphore_wait(ready_next, 1)
        to_below[1].start()

    @pl.when(rad > 0)
    def _():
        to_above[0].wait_recv()

    @pl.when(first)
    def _():
        for c in range(3):
            grid[c, 0] = grid[c, 1]

    step_in = length([grid[c, 1] for c in range(3)], [grid[c, 0] for c in range(3)])

    pl.when(rad != half)(far_last.wait_recv)

    @pl.when(rad == half)
    def _():
        for c in range(3):
            far_prior[c] = far_in[c]

    far_step = length([far_in[c] for c in range(3)], [far_prior[c] for c in range(3)])
    sums[place, 0] = step_in + top[3]
    sums[place, 1] = far_in[6] + far_step
    sum_sends = [
        send(sums.at[place], sums.at[place], (sum_s, sum_r), k, device)
        for k, device in enumerate(peers)
    ]
    for copy in sum_sends:
        copy.start()

    @pl.when(jnp.logical_not(turned))
    def _():
        for copy in bulk[AHEAD:]:
            copy.start()

    @pl.when(rad == half)
    def _():
        walls[0].wait_recv()
        for copy in passed:
            copy.start()

    loads[1].wait()

    def over_tan(j, packed):
        here = [flow[c, j + 2] for c in range(5)]
        m2, m1, p1, p2 = ([pltpu.roll(w, k, 1) for w in here] for k in (2, 1, 127, 126))
        odd, even = jst(m2, m1, here, p1, p2)
        for c in range(5):
            odd_t[c, j] = odd[c]
            even_t[c, j] = even[c]
        mine, shift = row_of == j, (4 * j + 2) % 128
        tight = [
            jnp.where(mine, pltpu.roll(here[c], shift, 1), packed[c]) for c in range(5)
        ]
        wide = [
            jnp.where(mine, pltpu.roll(jnp.where(lane < 64, p2[c], m2[c]), shift, 1), packed[c + 5])
            for c in range(5)
        ]
        return (*tight, *wide)

    packed = each_row(over_tan, (zero,) * 10)
    tight, wide = packed[:5], packed[5:]
    for c in range(5):
        edge_out[c] = tight[c]

    for load in loads[3:]:
        load.wait()
    own_id = jnp.where(inst == 0, ids_s[0], ids_s[1])
    other_id = jnp.where(inst == 0, ids_s[1], ids_s[0])
    offset_id = own_id - other_id
    turn = 2.0 * jnp.pi / NINST
    own_phase = turn * own_id.astype(jnp.float32) + motion_s[1]
    other_phase = turn * other_id.astype(jnp.float32) + motion_s[1]
    angle = (jnp.pi / NINST) * offset_id.astype(jnp.float32)
    angles = jnp.where(span == 0, own_phase, jnp.where(span == 1, other_phase, angle))
    sines, cosines = jnp.sin(angles), jnp.cos(angles)

    def pick(values, k):
        return jnp.broadcast_to(values[k : k + 1], TILE)

    theta = motion_s[0] * pick(sines, 0)
    sin_theta, cos_theta = jnp.sin(theta), jnp.cos(theta)
    own_far = [heave_s[c] * pick(cosines, 0) for c in range(3)]
    other_far = [heave_s[c] * pick(cosines, 1) for c in range(3)]
    parity = 1.0 - 2.0 * lax.rem(offset_id + NINST, 2).astype(jnp.float32)
    coef = 0.5 * parity * pick(cosines, 2) / pick(sines, 2)

    for copy in sum_sends:
        copy.wait_recv()
    own_half, other_half, lower = zero, zero, zero
    for k in range(half):
        own_half = own_half + sums[k, 0]
        other_half = other_half + sums[k, 1]
        lower = lower + jnp.where(k < place, sums[k, 0], 0.0)

    @pl.when(first)
    def _():
        for c in range(2):
            wall[c] = grid[c + 1, 1]

    @pl.when((rad != 0) & (rad != half))
    def _():
        for k in range(half - 1):

            @pl.when(place == k + 1)
            def _():
                walls[k + 1].wait_recv()

    @pl.when(rad < nrad - 1)
    def _():
        to_below[0].wait_recv()

    @pl.when(last)
    def _():
        for c in range(3):
            grid[c, ROWS + 1] = grid[c, ROWS]

    step_out = length([grid[c, ROWS + 1] for c in range(3)], [grid[c, ROWS] for c in range(3)])
    wall_y, wall_z = wall[0], wall[1]
    own_wall = [
        zero,
        wall_y * cos_theta - wall_z * sin_theta - wall_y,
        wall_y * sin_theta + wall_z * cos_theta - wall_z,
    ]
    frac_out[ROWS] = own_wall[1]
    frac_out[ROWS + 1] = own_wall[2]

    inverse = 1.0 / (own_half + other_half)
    offset = lower + jnp.where(side == 1, other_half, 0.0)
    base = offset + step_in

    def displaced(frac):
        return [
            frac * own_far[0],
            (1.0 - frac) * own_wall[1] + frac * own_far[1],
            (1.0 - frac) * own_wall[2] + frac * own_far[2],
        ]

    def move(j, edge):
        frac = (base + arc[j]) * inverse
        frac_out[j] = frac
        mine, shift = row_of == j, (4 * j + 2) % 128
        out = []
        for c, d in enumerate(displaced(frac)):
            disp_out[c, j] = d
            point = grid[c, j + 1] + d
            moved[c, j + 1] = point
            out.append(jnp.where(mine, pltpu.roll(point, shift, 1), edge[c]))
        return tuple(out)

    edges = each_row(move, (zero,) * 3)

    def slab(src, dst, sems, k):
        size = ROWS // PARTS
        part = pl.ds(k * size, size + (2 if k == PARTS - 1 else 0))
        return send(src.at[part], dst.at[part], sems, k, partner)

    frac_sends = [slab(frac_out, frac_in, (frac_s, frac_r), k) for k in range(PARTS)]
    for copy in frac_sends:
        copy.start()
    for c in range(3):
        edge_out[5 + c] = edges[c]
    edge_sends = [
        send(edge_out, edge_left, one, 0, right),
        send(edge_out, edge_right, one, 1, left),
    ]

    @pl.when(tan < ntan - 1)
    def _():
        pl.semaphore_wait(ready_right, 1)

    edge_sends[0].start()

    @pl.when(tan == 0)
    def _():
        pl.semaphore_wait(ready_left, 1)

    edge_sends[1].start()

    for c, d in enumerate(displaced(offset * inverse)):
        moved[c, 0] = grid[c, 0] + d
    for c, d in enumerate(displaced((base + top[3] + step_out) * inverse)):
        moved[c, ROWS + 1] = grid[c, ROWS + 1] + d

    @pl.when(first)
    def _():
        for c in range(3):
            moved[c, 0] = moved[c, 1]

    @pl.when(last)
    def _():
        for c in range(3):
            moved[c, ROWS + 1] = moved[c, ROWS]

    at_low, at_high = span == 0, span == 7
    span_scale = jnp.where(at_low | at_high, 1.0, 0.5)

    def slopes(j, packed):
        outer = first if j == 0 else last if j == ROWS - 1 else False
        scale = jnp.where(outer, 1.0, 0.5)
        t, r, z = [], [], []
        for c in range(3):
            here = moved[c, j + 1]
            t.append((pltpu.roll(here, 127, 1) - pltpu.roll(here, 1, 1)) * 0.5)
            r.append((moved[c, j + 2] - moved[c, j]) * scale)
            over = jnp.where(at_high, here, pltpu.roll(here, 7, 0))
            under = jnp.where(at_low, here, pltpu.roll(here, 1, 0))
            z.append((over - under) * span_scale)
            e_t[c, j] = t[c]
            e_r[c, j] = r[c]
        face = [
            z[1] * r[2] - z[2] * r[1],
            z[2] * r[0] - z[0] * r[2],
            z[0] * r[1] - z[1] * r[0],
        ]
        volume = t[0] * face[0] + t[1] * face[1] + t[2] * face[2]
        if j < RAW:
            vol_out[j] = volume
        else:
            for c in range(5):
                product_out[c, j - RAW] = volume * flow[c, j + 2]
        mine, shift = row_of == j, (4 * j + 2) % 128
        return tuple(
            jnp.where(mine, pltpu.roll(face[c], shift, 1), packed[c]) for c in range(3)
        )

    face = each_row(slopes, (zero,) * 3)
    vol_sends = [send(vol_out, vol_in, (vol_s, vol_r), 0, partner)] + [
        send(
            product_out.at[:, pl.ds(j - RAW, 4)],
            state_in.at[:, pl.ds(j, 4)],
            (vol_s, vol_r), 1 + (j - RAW) // 4, partner,
        )
        for j in range(RAW, ROWS, 4)
    ]
    vol_sends[0].start()

    @pl.when(turned)
    def _():
        for copy in vol_sends[1:]:
            copy.start()

    for copy in edge_sends:
        copy.wait_recv()
    beside = [jnp.where(slot < 2, edge_left[c], edge_right[c]) for c in range(8)]
    rim = []
    for c in range(3):
        ahead = pltpu.roll(jnp.where(slot == 2, beside[5 + c], edges[c]), 127, 1)
        behind = pltpu.roll(jnp.where(slot == 1, beside[5 + c], edges[c]), 1, 1)
        rim.append((ahead - behind) * 0.5)
    rim_vol = rim[0] * face[0] + rim[1] * face[1] + rim[2] * face[2]
    for c in range(5):
        rim_out[c] = rim_vol * tight[c]
    rim_send = send(rim_out, rim_in, one, 3, partner)
    rim_send.start()

    @pl.when(jnp.logical_not(turned))
    def _():
        for copy in vol_sends[1:]:
            copy.start()
    m1, p1, m2, p2 = [], [], [], []
    for c in range(5):
        m2.append(jnp.where(slot < 2, wide[c], pltpu.roll(beside[c], 2, 1)))
        p2.append(jnp.where(slot < 2, pltpu.roll(beside[c], 126, 1), wide[c]))
        near = pltpu.roll(jnp.where(slot == 1, beside[c], tight[c]), 1, 1)
        m1.append(jnp.where(slot == 0, pltpu.roll(wide[c], 127, 1), near))
        near = pltpu.roll(jnp.where(slot == 2, beside[c], tight[c]), 127, 1)
        p1.append(jnp.where(slot == 3, pltpu.roll(wide[c], 1, 1), near))
    rim_odd, rim_even = jst(m2, m1, tight, p1, p2)

    @pl.when(rad > 0)
    def _():
        to_above[1].wait_recv()

    @pl.when(first)
    def _():
        flow[:, 0:2] = jnp.zeros((5, 2, *TILE), jnp.float32)

    @pl.when(rad < nrad - 1)
    def _():
        to_below[1].wait_recv()

    @pl.when(last)
    def _():
        flow[:, ROWS + 2 : ROWS + 4] = jnp.zeros((5, 2, *TILE), jnp.float32)

    def over_rad(j, carry):
        odd, even = jst(*([flow[c, j + k] for c in range(5)] for k in range(5)))
        for c in range(5):
            odd_r[c, j] = odd[c]
            even_r[c, j] = even[c]
        return carry

    lax.fori_loop(0, ROWS, over_rad, 0, unroll=2)

    loads[2].wait()
    for copy in frac_sends:
        copy.wait_recv()
    other_wall = [zero, frac_in[ROWS], frac_in[ROWS + 1]]
    start = [stream_s[c] - coef * other_wall[c] for c in range(3)]
    slope = [coef * (other_wall[c] - other_far[c]) for c in range(3)]
    outer_two = (lane < 2) | (lane > 125)
    outer_one = (lane == 0) | (lane == 127)

    def fluxes(j, carry):
        shift = (126 - 4 * j) % 128
        frac = frac_in[j]
        relative = [start[c] + frac * slope[c] for c in range(3)]
        tangent = [jnp.where(outer_one, pltpu.roll(rim[c], shift, 1), e_t[c, j]) for c in range(3)]
        speed_t = sum(relative[c] * tangent[c] for c in range(3))
        speed_r = sum(relative[c] * e_r[c, j] for c in range(3))
        size_t, size_r = jnp.abs(speed_t), jnp.abs(speed_r)
        for c in range(5):
            odd = jnp.where(outer_two, pltpu.roll(rim_odd[c], shift, 1), odd_t[c, j])
            even = jnp.where(outer_two, pltpu.roll(rim_even[c], shift, 1), even_t[c, j])
            over_t = speed_t * odd - size_t * even
            over_r = speed_r * odd_r[c, j] - size_r * even_r[c, j]
            res_out[c, j] = over_t + over_r + rest_v[c, j]
        return carry

    each_row(fluxes, 0)

    within = jnp.where(outer_one, 0.0, coef)
    for copy in bulk + vol_sends[:1]:
        copy.wait_recv()
    for j in range(RAW):
        weight = within * vol_in[j]
        for c in range(5):
            res_out[c, j] = res_out[c, j] + weight * state_in[c, j]
    rim_send.wait_recv()
    for c in range(5):
        rim_in[c] = coef * rim_in[c]
    for j in range(ROWS):
        for c in range(5):
            edge = pltpu.roll(rim_in[c], (126 - 4 * j) % 128, 1)
            res_out[c, j] = res_out[c, j] + jnp.where(outer_one, edge, 0.0)
    for j in range(RAW, ROWS):
        if j % 4 == 0:
            vol_sends[1 + (j - RAW) // 4].wait_recv()
        for c in range(5):
            res_out[c, j] = res_out[c, j] + within * state_in[c, j]

    @pl.when(rad < nrad - 1)
    def _():
        for copy in to_above:
            copy.wait_send()

    pl.when((rad > 0) & (rad != half))(to_below[0].wait_send)
    pl.when(first)(far_first.wait_send)
    pl.when(rad > 0)(to_below[1].wait_send)

    @pl.when(first)
    def _():
        for copy in walls:
            copy.wait_send()

    @pl.when(rad == half)
    def _():
        for copy in passed:
            copy.wait_send()

    pl.when(place < half - 1)(far_last.wait_send)
    pl.when(rad == half - 1)(near_last.wait_send)

    for copy in sum_sends + [far, rim_send] + edge_sends + frac_sends + vol_sends + bulk:
        copy.wait_send()


def store_kernel(disp, res, disp_out, res_out, sems):
    copies = [
        pltpu.make_async_copy(disp, disp_out.at[0], sems.at[0]),
        pltpu.make_async_copy(res, res_out.at[0], sems.at[1]),
    ]
    for copy in copies:
        copy.start()
    for copy in copies:
        copy.wait()


def body(nrad, ntan, *args):
    half = nrad // 2
    f32 = jnp.float32
    vmem, hbm = pltpu.VMEM, pltpu.HBM

    def tiles(*lead):
        return pltpu.VMEM((*lead, *TILE), f32)

    dma = pltpu.SemaphoreType.DMA
    scratch = [
        tiles(3, ROWS + 2), tiles(5, ROWS + 4), tiles(5, ROWS), tiles(3, ROWS + 2), tiles(ROWS),
        tiles(ROWS + 2), tiles(ROWS + 2), tiles(3, ROWS), tiles(3, ROWS), tiles(RAW), tiles(RAW), tiles(5, ROWS - RAW),
        tiles(5, ROWS), tiles(5, ROWS), tiles(5, ROWS), tiles(5, ROWS), tiles(5, ROWS),
        tiles(2), tiles(half, 2), tiles(7), tiles(7), tiles(3), tiles(8), tiles(8), tiles(8), tiles(5), tiles(5),
        pltpu.SMEM((2,), jnp.int32), pltpu.SMEM((2,), f32), pltpu.SMEM((3,), f32), pltpu.SMEM((3,), f32),
        dma((7,)), dma((len(CUTS) - 1,)), dma((len(CUTS) - 1,)), dma((4,)), dma((4,)),
        dma((half,)), dma((half,)), dma((half - 1,)), dma((half - 1,)), dma((5,)), dma((5,)),
        dma((PARTS,)), dma((PARTS,)), dma((1 + (ROWS - RAW) // 4,)), dma((1 + (ROWS - RAW) // 4,)),
        *[pltpu.SemaphoreType.REGULAR] * 4,
    ]
    disp, res = pl.pallas_call(
        functools.partial(step_kernel, nrad, ntan),
        out_shape=[
            jax.ShapeDtypeStruct((3, ROWS, *TILE), f32),
            jax.ShapeDtypeStruct((5, ROWS, *TILE), f32),
        ],
        in_specs=[pl.BlockSpec(memory_space=hbm)] * 7,
        out_specs=[pl.BlockSpec(memory_space=vmem)] * 2,
        scratch_shapes=scratch,
        name="deform_and_residual",
        compiler_params=pltpu.CompilerParams(
            collective_id=0, has_side_effects=True, vmem_limit_bytes=24 * 2**20
        ),
    )(*(pltpu.with_memory_space_constraint(arg, hbm) for arg in args))
    return pl.pallas_call(
        store_kernel,
        out_shape=[
            jax.ShapeDtypeStruct((1, 3, ROWS, *TILE), f32),
            jax.ShapeDtypeStruct((1, 5, ROWS, *TILE), f32),
        ],
        in_specs=[pl.BlockSpec(memory_space=vmem)] * 2,
        out_specs=[pl.BlockSpec(memory_space=hbm)] * 2,
        scratch_shapes=[dma((2,))],
        name="store_results",
    )(*(pltpu.with_memory_space_constraint(x, vmem) for x in (disp, res)))


def solution(mesh):
    split = P("inst", None, "rad", None, "tan")
    return jax.shard_map(
        functools.partial(body, mesh.shape["rad"], mesh.shape["tan"]),
        mesh=mesh,
        in_specs=(split, split, split, P(), P(), P(), P()),
        out_specs=(split, split),
        check_vma=False,
    )
```

```python
import functools

import jax
import jax.numpy as jnp
from jax import lax
from jax.experimental import pallas as pl
from jax.experimental.pallas import tpu as pltpu
from jax.sharding import PartitionSpec as P

NINST = 16
COEF_TWO = 0.1
COEF_FOUR = 0.05
MESH = pl.DeviceIdType.MESH
ROWS = 32
RAW = 24
CUTS = (0, 2, 8, 14, 20, RAW)
AHEAD = 3
PARTS = 4
TILE = (8, 128)


def send(src, dst, sems, slot, device):
    return pltpu.make_async_remote_copy(
        src_ref=src,
        dst_ref=dst,
        send_sem=sems[0].at[slot],
        recv_sem=sems[1].at[slot],
        device_id=device,
        device_id_type=MESH,
    )


def length(a, b):
    d = [p - q for p, q in zip(a, b)]
    return jnp.sqrt(d[0] * d[0] + d[1] * d[1] + d[2] * d[2])


def each_row(body, carry):
    for j in range(ROWS):
        carry = body(j, carry)
    return carry


def jst(m2, m1, c, p1, p2):
    q_m, q_c, q_p = (1.0 + w[0] * w[0] for w in (m1, c, p1))
    outer = q_p + q_m
    sensor = COEF_TWO * jnp.abs(outer - 2.0 * q_c) / (outer + 2.0 * q_c)
    fourth = jnp.maximum(0.0, COEF_FOUR - sensor)
    near = sensor + 4.0 * fourth
    mid = 2.0 * sensor + 6.0 * fourth
    odd = [0.5 * (p1[k] - m1[k]) for k in range(5)]
    even = [near * (p1[k] + m1[k]) - mid * c[k] - fourth * (p2[k] + m2[k]) for k in range(5)]
    return odd, even


def step_kernel(
    nrad, ntan,
    coords, state, rest, ids, motion, heave, stream,
    disp_out, res_out,
    grid, flow, rest_v, moved, arc, frac_out, frac_in, e_t, e_r, vol_out, vol_in, product_out, state_in,
    odd_t, even_t, odd_r, even_r,
    wall, sums, far_out, far_in, far_prior, edge_out, edge_left, edge_right, rim_out, rim_in,
    ids_s, motion_s, heave_s, stream_s,
    local, bulk_s, bulk_r, row_s, row_r, wall_s, wall_r, sum_s, sum_r, one_s, one_r,
    frac_s, frac_r, vol_s, vol_r, ready_rad, ready_next, ready_right, ready_left,
):
    rad, tan, inst = lax.axis_index("rad"), lax.axis_index("tan"), lax.axis_index("inst")
    half = nrad // 2
    place, side = lax.rem(rad, half), rad // half
    first, last = rad == 0, rad == nrad - 1
    partner = {"inst": 1 - inst}
    left = {"tan": lax.rem(tan + ntan - 1, ntan)}
    right = {"tan": lax.rem(tan + 1, ntan)}
    above = {"rad": lax.rem(rad + 1, nrad)}
    below = {"rad": lax.rem(rad + nrad - 1, nrad)}
    across = {"rad": lax.rem(rad + half, nrad)}
    peers = [{"rad": side * half + lax.rem(place + k, half)} for k in range(1, half)]

    loads = [
        pltpu.make_async_copy(coords.at[0], grid.at[:, pl.ds(1, ROWS)], local.at[0]),
        pltpu.make_async_copy(state.at[0], flow.at[:, pl.ds(2, ROWS)], local.at[1]),
        pltpu.make_async_copy(rest.at[0], rest_v, local.at[2]),
        pltpu.make_async_copy(ids, ids_s, local.at[3]),
        pltpu.make_async_copy(motion, motion_s, local.at[4]),
        pltpu.make_async_copy(heave, heave_s, local.at[5]),
        pltpu.make_async_copy(stream, stream_s, local.at[6]),
    ]
    barrier = pltpu.get_barrier_semaphore()
    turned = tan == 0

    def signal(semaphore, device, condition=None):
        def run():
            pl.semaphore_signal(semaphore, inc=1, device_id=device, device_id_type=MESH)

        run() if condition is None else pl.when(condition)(run)

    signal(barrier, partner)
    signal(barrier, across)
    for k, device in enumerate(peers):
        lower = place + k + 1 >= half
        signal(barrier, device, (lower & turned) | jnp.logical_not(lower | turned))
    signal(barrier, below, rad == half)
    signal(barrier, right, tan < ntan - 1)
    signal(barrier, left, turned)
    for load in loads:
        load.start()

    lane = lax.broadcasted_iota(jnp.int32, TILE, 1)
    span = lax.broadcasted_iota(jnp.int32, TILE, 0)
    zero = jnp.zeros(TILE, jnp.float32)
    row_of, slot = lane // 4, lax.rem(lane, 4)

    awaited = jnp.where(turned, half - 1 - place, place)
    higher = jnp.where(tan > 0, 1, 0) + jnp.where(tan == ntan - 1, 1, 0)
    pl.semaphore_wait(barrier, 2 + awaited + jnp.where(rad == half - 1, 1, 0) + higher)
    for k, device in enumerate(peers):
        lower = place + k + 1 >= half
        signal(ready_rad, device, (lower & jnp.logical_not(turned)) | (turned & jnp.logical_not(lower)))
    signal(ready_next, above, rad == half - 1)
    signal(ready_right, left, tan > 0)
    signal(ready_left, right, tan == ntan - 1)

    one = (one_s, one_r)
    far = send(far_out, far_in, one, 2, across)
    far_last = send(far_in.at[pl.ds(3, 3)], far_prior, one, 4, above)
    near_last = send(coords.at[0, :, ROWS - 1], far_prior, one, 4, peers[0])
    row = (row_s, row_r)
    to_above = [
        send(coords.at[0, :, ROWS - 1], grid.at[:, 0], row, 0, above),
        send(state.at[0, :, pl.ds(ROWS - 2, 2)], flow.at[:, pl.ds(0, 2)], row, 1, above),
    ]
    to_below = [
        send(coords.at[0, :, 0], grid.at[:, ROWS + 1], row, 2, below),
        send(state.at[0, :, pl.ds(0, 2)], flow.at[:, pl.ds(ROWS + 2, 2)], row, 3, below),
    ]
    far_first = send(far_in.at[pl.ds(0, 3)], grid.at[:, ROWS + 1], row, 2, peers[-1])
    walls = [
        send(coords.at[0, pl.ds(1, 2), 0], wall, (wall_s, wall_r), k, device)
        for k, device in enumerate([across] + peers)
    ]
    passed = [send(wall, wall, (wall_s, wall_r), k + 1, device) for k, device in enumerate(peers)]
    bulk = [
        send(
            state.at[0, :, pl.ds(low, high - low)],
            state_in.at[:, pl.ds(low, high - low)],
            (bulk_s, bulk_r), k, partner,
        )
        for k, (low, high) in enumerate(zip(CUTS, CUTS[1:]))
    ]

    pl.when(turned & (place < half - 1))(to_above[0].start)
    bulk[0].start()
    pl.when(rad == half - 1)(to_above[0].start)
    pl.when(first)(walls[0].start)

    loads[0].wait()

    def inner(j, carry):
        before, total = carry[:3], carry[3]
        here = tuple(grid[c, j + 1] for c in range(3))
        total = total + length(here, before)
        arc[j] = total
        return (*here, total)

    arc[0] = zero
    top = lax.fori_loop(
        1, ROWS, inner, (*(grid[c, 1] for c in range(3)), zero), unroll=4
    )

    for c in range(3):
        far_out[c] = grid[c, 1]
        far_out[3 + c] = grid[c, ROWS]
    far_out[6] = top[3]
    far.start()
    pl.when(rad == half - 1)(to_above[1].start)
    for copy in bulk[1:AHEAD]:
        copy.start()

    @pl.when(turned)
    def _():
        for copy in bulk[AHEAD:]:
            copy.start()

    pl.when(awaited < half - 1)(
        lambda: pl.semaphore_wait(ready_rad, half - 1 - awaited)
    )

    pl.when((place < half - 1) & jnp.logical_not(turned))(to_above[0].start)
    pl.when(place < half - 1)(to_above[1].start)
    pl.when(rad == half - 1)(near_last.start)

    @pl.when(first)
    def _():
        for copy in walls[1:]:
            copy.start()

    @pl.when(place > 0)
    def _():
        for copy in to_below:
            copy.start()

    for load in loads[3:]:
        load.wait()
    own_id = jnp.where(inst == 0, ids_s[0], ids_s[1])
    other_id = jnp.where(inst == 0, ids_s[1], ids_s[0])
    offset_id = own_id - other_id
    turn = 2.0 * jnp.pi / NINST
    own_phase = turn * own_id.astype(jnp.float32) + motion_s[1]
    other_phase = turn * other_id.astype(jnp.float32) + motion_s[1]
    angle = (jnp.pi / NINST) * offset_id.astype(jnp.float32)
    angles = jnp.where(span == 0, own_phase, jnp.where(span == 1, other_phase, angle))
    sines, cosines = jnp.sin(angles), jnp.cos(angles)

    def pick(values, k):
        return jnp.broadcast_to(values[k : k + 1], TILE)

    theta = motion_s[0] * pick(sines, 0)
    sin_theta, cos_theta = jnp.sin(theta), jnp.cos(theta)
    own_far = [heave_s[c] * pick(cosines, 0) for c in range(3)]
    other_far = [heave_s[c] * pick(cosines, 1) for c in range(3)]
    parity = 1.0 - 2.0 * lax.rem(offset_id + NINST, 2).astype(jnp.float32)
    coef = 0.5 * parity * pick(cosines, 2) / pick(sines, 2)

    far.wait_recv()
    pl.when(place < half - 1)(far_last.start)
    pl.when(first)(far_first.start)

    @pl.when(rad == half)
    def _():
        pl.semaphore_wait(ready_next, 1)
        to_below[1].start()

    @pl.when(rad > 0)
    def _():
        to_above[0].wait_recv()

    @pl.when(first)
    def _():
        for c in range(3):
            grid[c, 0] = grid[c, 1]

    step_in = length([grid[c, 1] for c in range(3)], [grid[c, 0] for c in range(3)])

    pl.when(rad != half)(far_last.wait_recv)

    @pl.when(rad == half)
    def _():
        for c in range(3):
            far_prior[c] = far_in[c]

    far_step = length([far_in[c] for c in range(3)], [far_prior[c] for c in range(3)])
    sums[place, 0] = step_in + top[3]
    sums[place, 1] = far_in[6] + far_step
    sum_sends = [
        send(sums.at[place], sums.at[place], (sum_s, sum_r), k, device)
        for k, device in enumerate(peers)
    ]
    for copy in sum_sends:
        copy.start()

    @pl.when(jnp.logical_not(turned))
    def _():
        for copy in bulk[AHEAD:]:
            copy.start()

    @pl.when(rad == half)
    def _():
        walls[0].wait_recv()
        for copy in passed:
            copy.start()

    loads[1].wait()

    def over_tan(j, packed):
        here = [flow[c, j + 2] for c in range(5)]
        m2, m1, p1, p2 = ([pltpu.roll(w, k, 1) for w in here] for k in (2, 1, 127, 126))
        odd, even = jst(m2, m1, here, p1, p2)
        for c in range(5):
            odd_t[c, j] = odd[c]
            even_t[c, j] = even[c]
        mine, shift = row_of == j, (4 * j + 2) % 128
        tight = [
            jnp.where(mine, pltpu.roll(here[c], shift, 1), packed[c]) for c in range(5)
        ]
        wide = [
            jnp.where(mine, pltpu.roll(jnp.where(lane < 64, p2[c], m2[c]), shift, 1), packed[c + 5])
            for c in range(5)
        ]
        return (*tight, *wide)

    packed = each_row(over_tan, (zero,) * 10)
    tight, wide = packed[:5], packed[5:]
    for c in range(5):
        edge_out[c] = tight[c]

    for copy in sum_sends:
        copy.wait_recv()
    own_half, other_half, lower = zero, zero, zero
    for k in range(half):
        own_half = own_half + sums[k, 0]
        other_half = other_half + sums[k, 1]
        lower = lower + jnp.where(k < place, sums[k, 0], 0.0)

    @pl.when(first)
    def _():
        for c in range(2):
            wall[c] = grid[c + 1, 1]

    @pl.when((rad != 0) & (rad != half))
    def _():
        for k in range(half - 1):

            @pl.when(place == k + 1)
            def _():
                walls[k + 1].wait_recv()

    @pl.when(rad < nrad - 1)
    def _():
        to_below[0].wait_recv()

    @pl.when(last)
    def _():
        for c in range(3):
            grid[c, ROWS + 1] = grid[c, ROWS]

    step_out = length([grid[c, ROWS + 1] for c in range(3)], [grid[c, ROWS] for c in range(3)])
    wall_y, wall_z = wall[0], wall[1]
    own_wall = [
        zero,
        wall_y * cos_theta - wall_z * sin_theta - wall_y,
        wall_y * sin_theta + wall_z * cos_theta - wall_z,
    ]
    frac_out[ROWS] = own_wall[1]
    frac_out[ROWS + 1] = own_wall[2]

    inverse = 1.0 / (own_half + other_half)
    offset = lower + jnp.where(side == 1, other_half, 0.0)
    base = offset + step_in

    def displaced(frac):
        return [
            frac * own_far[0],
            (1.0 - frac) * own_wall[1] + frac * own_far[1],
            (1.0 - frac) * own_wall[2] + frac * own_far[2],
        ]

    def move(j, edge):
        frac = (base + arc[j]) * inverse
        frac_out[j] = frac
        mine, shift = row_of == j, (4 * j + 2) % 128
        out = []
        for c, d in enumerate(displaced(frac)):
            disp_out[c, j] = d
            point = grid[c, j + 1] + d
            moved[c, j + 1] = point
            out.append(jnp.where(mine, pltpu.roll(point, shift, 1), edge[c]))
        return tuple(out)

    edges = each_row(move, (zero,) * 3)

    def slab(src, dst, sems, k):
        size = ROWS // PARTS
        part = pl.ds(k * size, size + (2 if k == PARTS - 1 else 0))
        return send(src.at[part], dst.at[part], sems, k, partner)

    frac_sends = [slab(frac_out, frac_in, (frac_s, frac_r), k) for k in range(PARTS)]
    for copy in frac_sends:
        copy.start()
    for c in range(3):
        edge_out[5 + c] = edges[c]
    edge_sends = [
        send(edge_out, edge_left, one, 0, right),
        send(edge_out, edge_right, one, 1, left),
    ]

    @pl.when(tan < ntan - 1)
    def _():
        pl.semaphore_wait(ready_right, 1)

    edge_sends[0].start()

    @pl.when(tan == 0)
    def _():
        pl.semaphore_wait(ready_left, 1)

    edge_sends[1].start()

    for c, d in enumerate(displaced(offset * inverse)):
        moved[c, 0] = grid[c, 0] + d
    for c, d in enumerate(displaced((base + top[3] + step_out) * inverse)):
        moved[c, ROWS + 1] = grid[c, ROWS + 1] + d

    @pl.when(first)
    def _():
        for c in range(3):
            moved[c, 0] = moved[c, 1]

    @pl.when(last)
    def _():
        for c in range(3):
            moved[c, ROWS + 1] = moved[c, ROWS]

    at_low, at_high = span == 0, span == 7
    span_scale = jnp.where(at_low | at_high, 1.0, 0.5)

    def slopes(j, packed):
        outer = first if j == 0 else last if j == ROWS - 1 else False
        scale = jnp.where(outer, 1.0, 0.5)
        t, r, z = [], [], []
        for c in range(3):
            here = moved[c, j + 1]
            t.append((pltpu.roll(here, 127, 1) - pltpu.roll(here, 1, 1)) * 0.5)
            r.append((moved[c, j + 2] - moved[c, j]) * scale)
            over = jnp.where(at_high, here, pltpu.roll(here, 7, 0))
            under = jnp.where(at_low, here, pltpu.roll(here, 1, 0))
            z.append((over - under) * span_scale)
            e_t[c, j] = t[c]
            e_r[c, j] = r[c]
        face = [
            z[1] * r[2] - z[2] * r[1],
            z[2] * r[0] - z[0] * r[2],
            z[0] * r[1] - z[1] * r[0],
        ]
        volume = t[0] * face[0] + t[1] * face[1] + t[2] * face[2]
        if j < RAW:
            vol_out[j] = volume
        else:
            for c in range(5):
                product_out[c, j - RAW] = volume * flow[c, j + 2]
        mine, shift = row_of == j, (4 * j + 2) % 128
        return tuple(
            jnp.where(mine, pltpu.roll(face[c], shift, 1), packed[c]) for c in range(3)
        )

    face = each_row(slopes, (zero,) * 3)
    vol_sends = [send(vol_out, vol_in, (vol_s, vol_r), 0, partner)] + [
        send(
            product_out.at[:, pl.ds(j - RAW, 4)],
            state_in.at[:, pl.ds(j, 4)],
            (vol_s, vol_r), 1 + (j - RAW) // 4, partner,
        )
        for j in range(RAW, ROWS, 4)
    ]
    vol_sends[0].start()

    @pl.when(turned)
    def _():
        for copy in vol_sends[1:]:
            copy.start()

    for copy in edge_sends:
        copy.wait_recv()
    beside = [jnp.where(slot < 2, edge_left[c], edge_right[c]) for c in range(8)]
    rim = []
    for c in range(3):
        ahead = pltpu.roll(jnp.where(slot == 2, beside[5 + c], edges[c]), 127, 1)
        behind = pltpu.roll(jnp.where(slot == 1, beside[5 + c], edges[c]), 1, 1)
        rim.append((ahead - behind) * 0.5)
    rim_vol = rim[0] * face[0] + rim[1] * face[1] + rim[2] * face[2]
    for c in range(5):
        rim_out[c] = rim_vol * tight[c]
    rim_send = send(rim_out, rim_in, one, 3, partner)
    rim_send.start()

    @pl.when(jnp.logical_not(turned))
    def _():
        for copy in vol_sends[1:]:
            copy.start()
    m1, p1, m2, p2 = [], [], [], []
    for c in range(5):
        m2.append(jnp.where(slot < 2, wide[c], pltpu.roll(beside[c], 2, 1)))
        p2.append(jnp.where(slot < 2, pltpu.roll(beside[c], 126, 1), wide[c]))
        near = pltpu.roll(jnp.where(slot == 1, beside[c], tight[c]), 1, 1)
        m1.append(jnp.where(slot == 0, pltpu.roll(wide[c], 127, 1), near))
        near = pltpu.roll(jnp.where(slot == 2, beside[c], tight[c]), 127, 1)
        p1.append(jnp.where(slot == 3, pltpu.roll(wide[c], 1, 1), near))
    rim_odd, rim_even = jst(m2, m1, tight, p1, p2)

    @pl.when(rad > 0)
    def _():
        to_above[1].wait_recv()

    @pl.when(first)
    def _():
        flow[:, 0:2] = jnp.zeros((5, 2, *TILE), jnp.float32)

    @pl.when(rad < nrad - 1)
    def _():
        to_below[1].wait_recv()

    @pl.when(last)
    def _():
        flow[:, ROWS + 2 : ROWS + 4] = jnp.zeros((5, 2, *TILE), jnp.float32)

    def over_rad(j, carry):
        odd, even = jst(*([flow[c, j + k] for c in range(5)] for k in range(5)))
        for c in range(5):
            odd_r[c, j] = odd[c]
            even_r[c, j] = even[c]
        return carry

    lax.fori_loop(0, ROWS, over_rad, 0, unroll=2)

    loads[2].wait()
    for copy in frac_sends:
        copy.wait_recv()
    other_wall = [zero, frac_in[ROWS], frac_in[ROWS + 1]]
    start = [stream_s[c] - coef * other_wall[c] for c in range(3)]
    slope = [coef * (other_wall[c] - other_far[c]) for c in range(3)]
    outer_two = (lane < 2) | (lane > 125)
    outer_one = (lane == 0) | (lane == 127)

    def fluxes(j, carry):
        shift = (126 - 4 * j) % 128
        frac = frac_in[j]
        relative = [start[c] + frac * slope[c] for c in range(3)]
        tangent = [jnp.where(outer_one, pltpu.roll(rim[c], shift, 1), e_t[c, j]) for c in range(3)]
        speed_t = sum(relative[c] * tangent[c] for c in range(3))
        speed_r = sum(relative[c] * e_r[c, j] for c in range(3))
        size_t, size_r = jnp.abs(speed_t), jnp.abs(speed_r)
        for c in range(5):
            odd = jnp.where(outer_two, pltpu.roll(rim_odd[c], shift, 1), odd_t[c, j])
            even = jnp.where(outer_two, pltpu.roll(rim_even[c], shift, 1), even_t[c, j])
            over_t = speed_t * odd - size_t * even
            over_r = speed_r * odd_r[c, j] - size_r * even_r[c, j]
            res_out[c, j] = over_t + over_r + rest_v[c, j]
        return carry

    each_row(fluxes, 0)

    within = jnp.where(outer_one, 0.0, coef)
    for copy in bulk + vol_sends[:1]:
        copy.wait_recv()
    for j in range(RAW):
        weight = within * vol_in[j]
        for c in range(5):
            res_out[c, j] = res_out[c, j] + weight * state_in[c, j]
    rim_send.wait_recv()
    for c in range(5):
        rim_in[c] = coef * rim_in[c]
    for j in range(ROWS):
        for c in range(5):
            edge = pltpu.roll(rim_in[c], (126 - 4 * j) % 128, 1)
            res_out[c, j] = res_out[c, j] + jnp.where(outer_one, edge, 0.0)
    for j in range(RAW, ROWS):
        if j % 4 == 0:
            vol_sends[1 + (j - RAW) // 4].wait_recv()
        for c in range(5):
            res_out[c, j] = res_out[c, j] + within * state_in[c, j]

    @pl.when(rad < nrad - 1)
    def _():
        for copy in to_above:
            copy.wait_send()

    pl.when((rad > 0) & (rad != half))(to_below[0].wait_send)
    pl.when(first)(far_first.wait_send)
    pl.when(rad > 0)(to_below[1].wait_send)

    @pl.when(first)
    def _():
        for copy in walls:
            copy.wait_send()

    @pl.when(rad == half)
    def _():
        for copy in passed:
            copy.wait_send()

    pl.when(place < half - 1)(far_last.wait_send)
    pl.when(rad == half - 1)(near_last.wait_send)

    for copy in sum_sends + [far, rim_send] + edge_sends + frac_sends + vol_sends + bulk:
        copy.wait_send()


def store_kernel(disp, res, disp_out, res_out, sems):
    copies = [
        pltpu.make_async_copy(disp, disp_out.at[0], sems.at[0]),
        pltpu.make_async_copy(res, res_out.at[0], sems.at[1]),
    ]
    for copy in copies:
        copy.start()
    for copy in copies:
        copy.wait()


def body(nrad, ntan, *args):
    half = nrad // 2
    f32 = jnp.float32
    vmem, hbm = pltpu.VMEM, pltpu.HBM

    def tiles(*lead):
        return pltpu.VMEM((*lead, *TILE), f32)

    dma = pltpu.SemaphoreType.DMA
    scratch = [
        tiles(3, ROWS + 2), tiles(5, ROWS + 4), tiles(5, ROWS), tiles(3, ROWS + 2), tiles(ROWS),
        tiles(ROWS + 2), tiles(ROWS + 2), tiles(3, ROWS), tiles(3, ROWS), tiles(RAW), tiles(RAW), tiles(5, ROWS - RAW),
        tiles(5, ROWS), tiles(5, ROWS), tiles(5, ROWS), tiles(5, ROWS), tiles(5, ROWS),
        tiles(2), tiles(half, 2), tiles(7), tiles(7), tiles(3), tiles(8), tiles(8), tiles(8), tiles(5), tiles(5),
        pltpu.SMEM((2,), jnp.int32), pltpu.SMEM((2,), f32), pltpu.SMEM((3,), f32), pltpu.SMEM((3,), f32),
        dma((7,)), dma((len(CUTS) - 1,)), dma((len(CUTS) - 1,)), dma((4,)), dma((4,)),
        dma((half,)), dma((half,)), dma((half - 1,)), dma((half - 1,)), dma((5,)), dma((5,)),
        dma((PARTS,)), dma((PARTS,)), dma((1 + (ROWS - RAW) // 4,)), dma((1 + (ROWS - RAW) // 4,)),
        *[pltpu.SemaphoreType.REGULAR] * 4,
    ]
    disp, res = pl.pallas_call(
        functools.partial(step_kernel, nrad, ntan),
        out_shape=[
            jax.ShapeDtypeStruct((3, ROWS, *TILE), f32),
            jax.ShapeDtypeStruct((5, ROWS, *TILE), f32),
        ],
        in_specs=[pl.BlockSpec(memory_space=hbm)] * 7,
        out_specs=[pl.BlockSpec(memory_space=vmem)] * 2,
        scratch_shapes=scratch,
        name="deform_and_residual",
        compiler_params=pltpu.CompilerParams(
            collective_id=0, has_side_effects=True, vmem_limit_bytes=24 * 2**20
        ),
    )(*(pltpu.with_memory_space_constraint(arg, hbm) for arg in args))
    return pl.pallas_call(
        store_kernel,
        out_shape=[
            jax.ShapeDtypeStruct((1, 3, ROWS, *TILE), f32),
            jax.ShapeDtypeStruct((1, 5, ROWS, *TILE), f32),
        ],
        in_specs=[pl.BlockSpec(memory_space=vmem)] * 2,
        out_specs=[pl.BlockSpec(memory_space=hbm)] * 2,
        scratch_shapes=[dma((2,))],
        name="store_results",
    )(*(pltpu.with_memory_space_constraint(x, vmem) for x in (disp, res)))


def solution(mesh):
    split = P("inst", None, "rad", None, "tan")
    return jax.shard_map(
        functools.partial(body, mesh.shape["rad"], mesh.shape["tan"]),
        mesh=mesh,
        in_specs=(split, split, split, P(), P(), P(), P()),
        out_specs=(split, split),
        check_vma=False,
    )
```
